32 devices in a mesh: pipe: 4 (over y, core), head: 8 (over z, x).
Axes of the slice: x: 2, y: 2, z: 4, core: 2. Of those that a mesh axis runs over, the one named last changes fastest.
Arguments:
- patch_in: bfloat16 [4, 8, 2048], P(None, 'head'), may hold values from -200 to 200
- patch_start: int32 [4], replicated, may hold values from 0 to 2040, as said below
- mod_scale: float32 [4, 2048], P('pipe'), may hold values from -2.5 to 2.5
- mod_shift: float32 [4, 2048], P('pipe'), may hold values from -2.5 to 2.5
- res_gate: float32 [4, 2048], P('pipe'), may hold values from -4 to 4
- query_weight: bfloat16 [4, 16, 2048, 128], P('pipe', 'head'), may hold values from -0.3125 to 0.3125
- kv_weight: bfloat16 [4, 16, 2048, 256], P('pipe', 'head'), may hold values from -0.125 to 0.125
- stale_keys: bfloat16 [4, 16, 2048, 128], P('pipe', 'head'), may hold values from -3000 to 3000
- stale_values: bfloat16 [4, 16, 2048, 128], P('pipe', 'head'), may hold values from -6 to 6
Outputs:
- hidden_out: bfloat16 [4, 4, 8, 2048], P('pipe', None, 'head')
The draws below stay inside these ranges and needn't reach their ends.
Inputs may be any that keep to these rules, and one draw needn't show every extreme that they name: `patch_start`: distinct multiples of 8; the first and the last possible start are always among them.
All inputs are finite; a program needn't handle non-finite values.
Results may differ from the reference program's by a relative error of at most 0.035.
Values may be sent and summed in bfloat16 or wider, within the bound.
No kernel may reach another device: no remote copies, remote signals or barrier semaphores. Data moves between devices by JAX's collectives and lax.ppermute only.
A program may use at most 64 MiB of HBM per device.

```python
import math
import jax
import jax.numpy as jnp
from jax import lax

HEADS = 16
HEAD_DIM = 128
MICRO = 4
FEAT = 2048
KEY_SPLIT = 1
PATCH = 8
SEQ = 2048
SHARD_KEYS = 2048
KV_BLOCKS = 16
N_PIPE = 4


def draw_patch_in(key, part):
    key = jax.random.fold_in(key, 2)
    base_key = jax.random.fold_in(key, 0)
    shape = (MICRO, PATCH, FEAT)
    values = jnp.clip(jax.random.normal(base_key, shape, jnp.float32), -6.0, 6.0)
    return values.astype(jnp.bfloat16)


def draw_patch_start(key, part):
    key = jax.random.fold_in(key, 1)
    middle_key, order_key = jax.random.split(key)
    slots = SEQ // PATCH
    middle = jax.random.permutation(middle_key, slots - 2)[:MICRO - 2] + 1
    chosen = jnp.concatenate([jnp.array([0, slots - 1], jnp.int32), middle.astype(jnp.int32)])
    order = chosen[jax.random.permutation(order_key, MICRO)]
    return (order * PATCH).astype(jnp.int32)


def draw_stale_keys(key, part):
    key = jax.random.fold_in(key, 3)
    base_key = jax.random.fold_in(key, 0)
    shape = (N_PIPE, KV_BLOCKS, SHARD_KEYS, HEAD_DIM)
    base = jnp.clip(jax.random.normal(base_key, shape, jnp.float32), -6.0, 6.0)
    return base.astype(jnp.bfloat16)


def level_of(own_key, dims, pieces, least, high):
    gain, own = 1.0, jax.random.fold_in(own_key, 6)
    for position, parts in pieces:
        heights = jnp.exp(jax.random.uniform(jax.random.fold_in(own, position), (parts,), jnp.float32, least / len(pieces), high / len(pieces)))
        gain = gain * jnp.repeat(heights, dims[position] // parts).reshape([-1 if axis == position else 1 for axis in range(len(dims))])
    return gain


def centred(own_key, dims, scale, most, pieces=(), dtype=jnp.bfloat16):
    factor_of = level_of(own_key, dims, pieces, -0.22, 0.18) if pieces else 1.0
    result = jax.random.normal(own_key, dims, jnp.float32) * scale * factor_of
    return jnp.minimum(jnp.maximum(result, -most), most).astype(dtype)


def setup_inputs(seed: int = 0) -> dict:
    streams_of = jax.random.split(jax.random.key(seed), 10)
    return {
        "patch_in": draw_patch_in(jax.random.fold_in(streams_of[9], 71), 0),
        "patch_start": draw_patch_start(jax.random.fold_in(streams_of[9], 71), 0),
        "mod_scale": centred(streams_of[2], (N_PIPE, FEAT), 0.5, 2.5, ((0, 4),), jnp.float32),
        "mod_shift": centred(streams_of[3], (N_PIPE, FEAT), 0.5, 2.5, ((0, 4),), jnp.float32),
        "res_gate": centred(streams_of[4], (N_PIPE, FEAT), 1.0, 4.0, ((0, 4),), jnp.float32),
        "query_weight": centred(streams_of[5], (N_PIPE, KV_BLOCKS, FEAT // KEY_SPLIT, HEAD_DIM), (FEAT // 6) ** -0.5, 0.3125, ((0, 4), (1, 8))),
        "kv_weight": centred(streams_of[6], (N_PIPE, KV_BLOCKS, FEAT // KEY_SPLIT, 2 * HEAD_DIM), FEAT ** -0.5, 0.125, ((0, 4), (1, 8))),
        "stale_keys": draw_stale_keys(jax.random.fold_in(streams_of[9], 71), 0),
        "stale_values": centred(streams_of[8], (N_PIPE, KV_BLOCKS, SHARD_KEYS, HEAD_DIM), 1.0, 6.0, ((0, 4), (1, 8))),
    }


def modulate(rows, scale_row, shift_row):
    values = rows.astype(jnp.float32)
    meansq = lax.optimization_barrier(jnp.mean(values * values, axis=-1, keepdims=True))
    normed = values * lax.rsqrt(meansq + 1e-06)
    return (normed * (1.0 + scale_row) + shift_row).astype(jnp.bfloat16)

def attend_head(operands):
    query_per_head, keys_h, vals_h = operands
    head_dim = query_per_head.shape[-1]
    score_scale = 1.0 / math.sqrt(head_dim)
    key_block_list = keys_h.reshape(KEY_SPLIT, SHARD_KEYS, head_dim).astype(jnp.float32)
    value_block_list = vals_h.reshape(KEY_SPLIT, SHARD_KEYS, head_dim).astype(jnp.float32)
    logit_scores = jnp.einsum('tu,xvu->txv', query_per_head.astype(jnp.float32), key_block_list) * score_scale
    top = lax.optimization_barrier(jnp.max(logit_scores, axis=-1))
    expo = jnp.exp(logit_scores - top[..., None])
    total = lax.optimization_barrier(jnp.sum(expo, axis=-1))
    softmax_weight = lax.optimization_barrier(expo.astype(jnp.bfloat16)).astype(jnp.float32)
    blended_values = jnp.einsum('qzg,zgo->qzo', softmax_weight, value_block_list)
    part = blended_values / total[..., None]
    peak = lax.optimization_barrier(jnp.max(top, axis=1, keepdims=True))
    weight = jnp.exp(top - peak) * total
    return lax.optimization_barrier(jnp.sum(weight[..., None] * part, axis=1)) / lax.optimization_barrier(jnp.sum(weight, axis=1))[:, None]

def reference(patch_in, patch_start, mod_scale, mod_shift, res_gate, query_weight, kv_weight, stale_keys, stale_values):
    head_dim = query_weight.shape[3]
    current = [patch_in[index] for index in range(MICRO)]
    results = []
    for segment in range(N_PIPE):
        keys_cache = stale_keys[segment].reshape(HEADS, SEQ, head_dim)
        vals_cache = stale_values[segment].reshape(HEADS, SEQ, head_dim)
        wq = query_weight[segment].reshape(HEADS, FEAT, head_dim).astype(jnp.float32)
        wkv = kv_weight[segment].reshape(HEADS, FEAT, 2 * head_dim).astype(jnp.float32)
        segment_out = []
        for index in range(MICRO):
            tokens = current[index]
            modded = modulate(tokens, mod_scale[segment], mod_shift[segment]).astype(jnp.float32)
            query = jnp.einsum('pf,hfe->phe', modded, wq).astype(jnp.bfloat16)
            fresh = jnp.einsum('pf,hfe->phe', modded, wkv).astype(jnp.bfloat16)
            fresh_keys = jnp.transpose(fresh[..., :head_dim], (1, 0, 2))
            fresh_vals = jnp.transpose(fresh[..., head_dim:], (1, 0, 2))
            offset = patch_start[index].astype(jnp.int32)
            zero = jnp.zeros((), jnp.int32)
            keys_cache = lax.dynamic_update_slice(keys_cache, fresh_keys, (zero, offset, zero))
            vals_cache = lax.dynamic_update_slice(vals_cache, fresh_vals, (zero, offset, zero))
            per_head = lax.map(attend_head, (jnp.transpose(query, (1, 0, 2)), keys_cache, vals_cache))
            attn = jnp.transpose(per_head, (1, 0, 2)).reshape(PATCH, HEADS * head_dim)
            updated = (tokens.astype(jnp.float32) + res_gate[segment] * attn).astype(jnp.bfloat16)
            segment_out.append(updated)
        results.append(jnp.stack(segment_out))
        current = segment_out
    return jnp.stack(results)
```

```python
import functools
import math

import jax
import jax.numpy as jnp
from jax import lax
from jax.experimental import pallas as pl
from jax.experimental.pallas import tpu as pltpu
from jax.sharding import PartitionSpec as P

HEADS = 16
MASKED = -3.0e38


def layer_kernel(step, offsets, micro, patch, *refs):
    n_groups = len(offsets)
    start_ref, scale_ref, shift_ref, gate_ref, wq_ref, wkv_ref, key_ref, val_ref, held_ref = refs[:9]
    group_refs = refs[9 : 9 + n_groups]
    out_ref = refs[9 + n_groups]
    stage = lax.axis_index("pipe")
    head = lax.axis_index("head")
    heads_dev, feat, head_dim = wq_ref.shape
    positions = key_ref.shape[1]
    rows, width = out_ref.shape

    def column(offset):
        return pl.multiple_of(lax.bitwise_xor(head, offset) * width, width)

    @pl.when(stage != step)
    def _():
        out_ref[...] = held_ref[...]

    @pl.when(stage == step)
    def _():
        pieces = []
        for ref, group in zip(group_refs, offsets):
            for slot, offset in enumerate(group):
                if ref.shape[1] == feat:
                    at = column(offset)
                    pieces.append((at, ref[:, pl.ds(at, width)]))
                else:
                    pieces.append((column(offset), ref[slot * rows : (slot + 1) * rows, :]))
        square = None
        for _, piece in pieces:
            value = piece.astype(jnp.float32)
            square = value * value if square is None else square + value * value
        meansq = jnp.sum(square, axis=-1, keepdims=True) / feat
        inverse = lax.rsqrt(meansq + 1e-06)
        query = [None] * heads_dev
        fresh = [None] * heads_dev
        for at, piece in pieces:
            scale = 1.0 + scale_ref[:, pl.ds(at, width)]
            shift = shift_ref[:, pl.ds(at, width)]
            modded = (piece.astype(jnp.float32) * inverse * scale + shift).astype(jnp.bfloat16)
            for h in range(heads_dev):
                q = jnp.dot(modded, wq_ref[h, pl.ds(at, width), :], preferred_element_type=jnp.float32)
                kv = jnp.dot(modded, wkv_ref[h, pl.ds(at, width), :], preferred_element_type=jnp.float32)
                query[h] = q if query[h] is None else query[h] + q
                fresh[h] = kv if fresh[h] is None else fresh[h] + kv
        position = lax.broadcasted_iota(jnp.int32, (8, positions), 1)
        patch_row = lax.rem(lax.broadcasted_iota(jnp.int32, (8, positions), 0), micro)
        replaced = None
        for m in range(micro):
            relative = position - start_ref[m]
            inside = (relative >= 0) & (relative < patch) & (patch_row >= m)
            replaced = inside if replaced is None else replaced | inside
        asking = lax.rem(lax.broadcasted_iota(jnp.int32, (rows, rows), 0), micro)
        asked = lax.rem(lax.broadcasted_iota(jnp.int32, (rows, rows), 1), micro)
        later = asked > asking
        score_scale = 1.0 / math.sqrt(head_dim)
        over_last = (((1,), (1,)), ((), ()))
        attended = []
        for h in range(heads_dev):
            q = query[h].astype(jnp.bfloat16)
            k = fresh[h][:, :head_dim].astype(jnp.bfloat16)
            v = fresh[h][:, head_dim:].astype(jnp.bfloat16)
            old = lax.dot_general(q, key_ref[h], over_last, preferred_element_type=jnp.float32)
            old = old.reshape(rows // 8, 8, positions) * score_scale
            old = jnp.where(replaced[None], MASKED, old).reshape(rows, positions)
            new = lax.dot_general(q, k, over_last, preferred_element_type=jnp.float32)
            new = jnp.where(later, MASKED, new * score_scale)
            top = jnp.maximum(
                jnp.max(old, axis=-1, keepdims=True), jnp.max(new, axis=-1, keepdims=True)
            )
            old = jnp.exp(old - top)
            new = jnp.exp(new - top)
            total = jnp.sum(old, axis=-1, keepdims=True) + jnp.sum(new, axis=-1, keepdims=True)
            summed = jnp.dot(
                old.astype(jnp.bfloat16), val_ref[h], preferred_element_type=jnp.float32
            ) + jnp.dot(new.astype(jnp.bfloat16), v, preferred_element_type=jnp.float32)
            attended.append(summed / total)
        own = pl.multiple_of(head * width, width)
        residual = pieces[0][1].astype(jnp.float32)
        gate = gate_ref[:, pl.ds(own, width)]
        out_ref[...] = (residual + gate * jnp.concatenate(attended, axis=1)).astype(out_ref.dtype)


def run_layer(step, offsets, micro, patch, constants, held, groups):
    smem = pl.BlockSpec(memory_space=pltpu.SMEM)
    vmem = pl.BlockSpec(memory_space=pltpu.VMEM)
    return pl.pallas_call(
        functools.partial(layer_kernel, step, offsets, micro, patch),
        out_shape=jax.ShapeDtypeStruct(held.shape, held.dtype),
        in_specs=[smem] + [vmem] * (len(constants) + len(groups)),
        out_specs=vmem,
        compiler_params=pltpu.CompilerParams(vmem_limit_bytes=16 * 1024 * 1024),
    )(*constants, held, *groups)


def routed(value, route):
    n_pipe, n_head = lax.axis_size("pipe"), lax.axis_size("head")
    pairs = []
    for p in range(n_pipe):
        for h in range(n_head):
            to_pipe, to_head = route(p, h)
            pairs.append((p * n_head + h, to_pipe % n_pipe * n_head + to_head))
    return lax.ppermute(value, ("pipe", "head"), pairs)


def whole_heads(
    patch_in, patch_start, mod_scale, mod_shift, res_gate, query_weight, kv_weight, stale_keys, stale_values
):
    n_head = lax.axis_size("head")
    n_pipe = lax.axis_size("pipe")
    micro, rows_dev, feat = patch_in.shape
    heads_dev, head_dim = stale_keys.shape[1], stale_keys.shape[3]
    width = heads_dev * head_dim
    patch = rows_dev * n_head
    rows = micro * patch
    constants = (
        patch_start,
        mod_scale,
        mod_shift,
        res_gate,
        query_weight[0],
        kv_weight[0],
        stale_keys[0],
        stale_values[0],
    )
    mine = jnp.transpose(patch_in, (1, 0, 2)).reshape(rows // n_head, feat)
    copies = jnp.broadcast_to(mine[None], (n_head,) + mine.shape)
    gathered = lax.all_to_all(copies, "head", split_axis=0, concat_axis=0, tiled=True)
    held = jnp.zeros((rows, width), jnp.bfloat16)
    groups = [gathered.reshape(rows, feat)]
    offsets = [tuple(range(n_head))]
    for step in range(n_pipe):
        held = run_layer(step, offsets, micro, patch, constants, held, groups)
        if step + 1 < n_pipe:
            value = jnp.concatenate(
                [routed(held, lambda p, h: (p + 1, h)), routed(held, lambda p, h: (p + 1, h ^ 1))], 0
            )
            bit = 2
            while bit < n_head:
                value = jnp.concatenate([value, routed(value, lambda p, h: (p, h ^ bit))], 0)
                bit *= 2
            groups = [value]
    back = lax.all_to_all(
        held.reshape(n_head, rows // n_head, width), "head", split_axis=0, concat_axis=0, tiled=True
    )
    back = jnp.transpose(back.reshape(n_head, rows_dev, micro, width), (2, 1, 0, 3))
    return back.reshape(1, micro, rows_dev, feat)


def shifted(value, axis, steps):
    count = lax.axis_size(axis)
    leading, last = (max(0, -steps), min(count, count - steps))
    return lax.ppermute(value, axis, [(source, source + steps) for source in range(leading, last)])


def modulate(rows, scale_row, shift_row):
    values = rows.astype(jnp.float32)
    meansq = jnp.mean(values * values, axis=-1, keepdims=True)
    normed = values * lax.rsqrt(meansq + 1e-06)
    return (normed * (1.0 + scale_row) + shift_row).astype(jnp.bfloat16)


def feature_layout(modded, groups, splits):
    rows_dev, feat = modded.shape
    width = feat // splits
    pieces = jnp.transpose(modded.reshape(rows_dev, splits, width), (1, 0, 2))
    copies = jnp.broadcast_to(pieces[None], (groups, splits, rows_dev, width))
    return copies.reshape(groups * splits, rows_dev, width)


def project_partial(received, w_both):
    n_src, rows_dev, width = received.shape
    inputs = received.reshape(n_src * rows_dev, width)
    partial_sum = jnp.einsum("pf,hfe->phe", inputs, w_both, preferred_element_type=jnp.float32)
    return partial_sum.reshape(n_src, rows_dev, -1)


def sum_partials(returned, groups, splits, heads_dev):
    n_src, rows_dev, width = returned.shape
    triple = width // heads_dev
    summed = jnp.sum(returned.reshape(groups, splits, rows_dev, heads_dev, triple), axis=1)
    ordered = jnp.transpose(summed, (1, 0, 2, 3))
    return ordered.reshape(rows_dev, groups * heads_dev, triple).astype(jnp.bfloat16)


def head_layout(qkv_own, groups, splits):
    rows_dev, heads_all, triple = qkv_own.shape
    width = heads_all // groups * triple
    grouped = jnp.transpose(qkv_own.reshape(rows_dev, groups, width), (1, 0, 2))
    copies = jnp.broadcast_to(grouped[:, None], (groups, splits, rows_dev, width))
    return copies.reshape(groups * splits, rows_dev, width)


def attend_block(query_blk, keys_buf, vals_buf):
    score_scale = 1.0 / math.sqrt(query_blk.shape[-1])
    logit_scores = (
        jnp.einsum("qhd,hkd->hqk", query_blk, keys_buf, preferred_element_type=jnp.float32)
        * score_scale
    )
    top = jnp.max(logit_scores, axis=-1)
    expo = jnp.exp(logit_scores - top[..., None])
    total = jnp.sum(expo, axis=-1)
    softmax_weight = expo.astype(jnp.bfloat16)
    blended_values = jnp.einsum(
        "hqk,hkd->qhd", softmax_weight, vals_buf, preferred_element_type=jnp.float32
    )
    partial_out = blended_values / jnp.transpose(total)[..., None]
    return (partial_out, jnp.transpose(top), jnp.transpose(total))


def segment_attend(received, offset, keys_buf, vals_buf, key_base):
    heads_dev, shard_keys, head_dim = keys_buf.shape
    patch = received.shape[0] * received.shape[1]
    triples = received.reshape(patch, heads_dev, 3 * head_dim)
    query = triples[..., :head_dim]
    fresh = triples[..., head_dim:]
    position = key_base + jnp.arange(shard_keys, dtype=jnp.int32)
    relative = position - offset
    inside = ((relative >= 0) & (relative < patch))[None, :, None]
    picked = jnp.clip(relative, 0, patch - 1)
    taken = jnp.transpose(jnp.take(fresh, picked, axis=0), (1, 0, 2))
    new_keys = jnp.where(inside, taken[..., :head_dim], keys_buf)
    new_vals = jnp.where(inside, taken[..., head_dim:], vals_buf)
    block = min(512, patch)
    blocks = query.reshape(patch // block, block, heads_dev, head_dim)
    outs, tops, totals = lax.map(lambda blk: attend_block(blk, new_keys, new_vals), blocks)
    return (
        new_keys,
        new_vals,
        outs.reshape(patch, heads_dev, head_dim),
        tops.reshape(patch, heads_dev),
        totals.reshape(patch, heads_dev),
    )


def merge_parts(outs, tops, totals, groups, splits):
    n_dev, rows_dev, width = outs.shape
    heads_dev = tops.shape[-1]
    head_dim = width // heads_dev
    outs = outs.reshape(groups, splits, rows_dev, heads_dev, head_dim)
    tops = tops.reshape(groups, splits, rows_dev, heads_dev)
    totals = totals.reshape(groups, splits, rows_dev, heads_dev)
    peak = jnp.max(tops, axis=1, keepdims=True)
    weight = jnp.exp(tops - peak) * totals
    summed = jnp.sum(weight[..., None] * outs, axis=1) / jnp.sum(weight, axis=1)[..., None]
    return jnp.transpose(summed, (1, 0, 2, 3)).reshape(rows_dev, groups * width)


def per_device(
    patch_in,
    patch_start,
    mod_scale,
    mod_shift,
    res_gate,
    query_weight,
    kv_weight,
    stale_keys,
    stale_values,
):
    n_head = lax.axis_size("head")
    n_pipe = lax.axis_size("pipe")
    micro, rows_dev, feat = patch_in.shape
    heads_dev = stale_keys.shape[1]
    shard_keys = stale_keys.shape[2]
    head_dim = stale_keys.shape[3]
    splits = max(n_head // HEADS, 1)
    groups = n_head // splits
    patch = rows_dev * n_head
    head_index = lax.axis_index("head")
    segment = lax.axis_index("pipe")
    key_base = head_index % splits * shard_keys
    w_both = jnp.concatenate([query_weight[0], kv_weight[0]], axis=-1)
    scale_row = mod_scale[0]
    shift_row = mod_shift[0]
    gate_row = res_gate[0]

    def run_attention(valid, received, offset, keys_buf, vals_buf):

        def active(operands):
            return segment_attend(operands[0], operands[1], operands[2], operands[3], key_base)

        def resting(operands):
            return (
                operands[2],
                operands[3],
                jnp.zeros((patch, heads_dev, head_dim), jnp.float32),
                jnp.zeros((patch, heads_dev), jnp.float32),
                jnp.ones((patch, heads_dev), jnp.float32),
            )

        return lax.cond(valid, active, resting, (received, offset, keys_buf, vals_buf))

    def write_out(outputs, valid, index, updated):
        old = lax.dynamic_index_in_dim(outputs, index, 0, keepdims=False)
        return lax.dynamic_update_index_in_dim(outputs, jnp.where(valid, updated, old), index, 0)

    def entering(index, incoming):
        first = lax.dynamic_index_in_dim(patch_in, index, 0, keepdims=False)
        return jnp.where(segment == 0, first, incoming)

    outputs = jnp.zeros((micro, rows_dev, feat), jnp.bfloat16)
    incoming = jnp.zeros((rows_dev, feat), jnp.bfloat16)
    keys_buf = stale_keys[0]
    vals_buf = stale_values[0]

    def apart_step(step, carry):
        keys_buf, vals_buf, incoming, outputs = carry
        index = step - segment
        valid = (index >= 0) & (index < micro)
        safe = jnp.clip(index, 0, micro - 1)
        current = entering(safe, incoming)
        modded = modulate(current, scale_row, shift_row)
        recv_feat = lax.all_to_all(
            feature_layout(modded, groups, splits), "head", split_axis=0, concat_axis=0, tiled=True
        )
        partial_sum = project_partial(recv_feat, w_both)
        returned = lax.all_to_all(partial_sum, "head", split_axis=0, concat_axis=0, tiled=True)
        qkv_own = sum_partials(returned, groups, splits, heads_dev)
        recv_qkv = lax.all_to_all(
            head_layout(qkv_own, groups, splits), "head", split_axis=0, concat_axis=0, tiled=True
        )
        keys_buf, vals_buf, part_out, tops, totals = run_attention(
            valid, recv_qkv, patch_start[safe], keys_buf, vals_buf
        )
        outs_back, tops_back, totals_back = (
            lax.all_to_all(
                part_out.reshape(n_head, rows_dev, heads_dev * head_dim),
                "head",
                split_axis=0,
                concat_axis=0,
                tiled=True,
            ),
            lax.all_to_all(
                tops.reshape(n_head, rows_dev, heads_dev),
                "head",
                split_axis=0,
                concat_axis=0,
                tiled=True,
            ),
            lax.all_to_all(
                totals.reshape(n_head, rows_dev, heads_dev),
                "head",
                split_axis=0,
                concat_axis=0,
                tiled=True,
            ),
        )
        blended_values = merge_parts(outs_back, tops_back, totals_back, groups, splits)
        updated = (current.astype(jnp.float32) + gate_row * blended_values).astype(jnp.bfloat16)
        outputs = write_out(outputs, valid, safe, updated)
        incoming = shifted(updated, "pipe", 1)
        return (keys_buf, vals_buf, incoming, outputs)

    final = lax.fori_loop(
        0, micro + n_pipe - 1, apart_step, (keys_buf, vals_buf, incoming, outputs)
    )
    outputs = final[3]
    return outputs[None]


def solution(mesh):
    n_head = mesh.shape["head"]
    whole = n_head <= HEADS and n_head & (n_head - 1) == 0
    placed = (
        P(None, "head", None),
        P(),
        P("pipe", None),
        P("pipe", None),
        P("pipe", None),
        P("pipe", "head", None, None),
        P("pipe", "head", None, None),
        P("pipe", "head", None, None),
        P("pipe", "head", None, None),
    )
    return jax.shard_map(
        whole_heads if whole else per_device,
        mesh=mesh,
        in_specs=placed,
        out_specs=P("pipe", None, "head", None),
        check_vma=False,
    )
```

```python
import functools
import math

import jax
import jax.numpy as jnp
from jax import lax
from jax.experimental import pallas as pl
from jax.experimental.pallas import tpu as pltpu
from jax.sharding import PartitionSpec as P

HEADS = 16
MASKED = -3.0e38
LIMIT = 4 * 1024 * 1024
SMEM = pl.BlockSpec(memory_space=pltpu.SMEM)
VMEM = pl.BlockSpec(memory_space=pltpu.VMEM)
ANY = pl.BlockSpec(memory_space=pl.ANY)


def origin(head, kind, amount, count):
    if kind == "turn":
        return (head - amount + count) % count
    return head ^ amount


def traced(maps, head, count):
    for kind, amount in maps:
        head = origin(head, kind, amount, count)
    return head


def distinct(offsets, count):
    slots = {}
    for slot, maps in enumerate(offsets):
        slots.setdefault(tuple(traced(maps, head, count) for head in range(count)), (slot, maps))
    own = tuple(range(count))
    return [slots[own]] + [slots[key] for key in slots if key != own]


def routed(value, kind, amount, shift):
    n_pipe, n_head = lax.axis_size("pipe"), lax.axis_size("head")
    pairs = []
    for p in range(n_pipe):
        for h in range(n_head):
            source = p * n_head + origin(h, kind, amount, n_head)
            pairs.append((source, (p + shift) % n_pipe * n_head + h))
    return lax.ppermute(value, ("pipe", "head"), pairs)


def exchange(block, plan):
    value, offsets = block, [()]
    for shift, moves in plan:
        parts, known = [], []
        for kind, amount in moves:
            if shift == 0 and amount == 0:
                parts.append(value)
                known += offsets
            else:
                parts.append(routed(value, kind, amount, shift))
                known += [((kind, amount),) + maps for maps in offsets]
        value, offsets = jnp.concatenate(parts, 0), known
    return value, offsets


def load_kernel(micro, patch, start_ref, *refs):
    count = (len(refs) - 2) // 2
    sources, results = refs[:count], refs[count : 2 * count]
    hidden_ref, sems = refs[2 * count], refs[2 * count + 1]
    copies = [
        pltpu.make_async_copy(source, result, sems.at[index])
        for index, (source, result) in enumerate(zip(sources, results))
    ]
    for copy in copies:
        copy.start()
    position = lax.broadcasted_iota(jnp.int32, hidden_ref.shape, 1)
    patch_row = lax.rem(lax.broadcasted_iota(jnp.int32, hidden_ref.shape, 0), micro)
    hidden = jnp.zeros(hidden_ref.shape, jnp.int32)
    for m in range(micro):
        relative = position - start_ref[m]
        inside = (relative >= 0) & (relative < patch) & (patch_row >= m)
        hidden = jnp.where(inside, 1, hidden)
    hidden_ref[...] = hidden
    for copy in copies:
        copy.wait()


def load(patch_start, arrays, micro, patch, positions):
    shapes = [pltpu.VMEM(array.shape, array.dtype) for array in arrays]
    shapes.append(pltpu.VMEM((8, positions), jnp.int32))
    return pl.pallas_call(
        functools.partial(load_kernel, micro, patch),
        out_shape=shapes,
        in_specs=[SMEM] + [ANY] * len(arrays),
        out_specs=[VMEM] * len(shapes),
        scratch_shapes=[pltpu.SemaphoreType.DMA((len(arrays),))],
        compiler_params=pltpu.CompilerParams(vmem_limit_bytes=LIMIT),
        cost_estimate=pl.CostEstimate(flops=0, bytes_accessed=10 * 1024 * 1024, transcendentals=0),
    )(patch_start, *(pltpu.with_memory_space_constraint(array, pltpu.HBM) for array in arrays))


def layer_kernel(step, slots, micro, *refs):
    scale_ref, shift_ref, gate_ref, wq_ref, wkv_ref, key_ref, val_ref, hidden_ref, held_ref, in_ref = refs[:10]
    out_ref = refs[10]
    stage = lax.axis_index("pipe")
    head = lax.axis_index("head")
    n_head = lax.axis_size("head")
    heads_dev, feat, head_dim = wq_ref.shape
    positions = key_ref.shape[1]
    rows, width = held_ref.shape
    by_token = len(in_ref.shape) == 3
    own = pl.multiple_of(head * width, width)

    @pl.when(stage != step)
    def _():
        out_ref[...] = held_ref[...].reshape(out_ref.shape)

    @pl.when(stage == step)
    def _():
        pieces = []
        if by_token:
            for index in range(n_head):
                at = index * width
                pieces.append((at, in_ref[:, :, at : at + width].astype(jnp.float32).reshape(rows, width)))
            residual = in_ref[:, :, pl.ds(own, width)].astype(jnp.float32).reshape(rows, width)
        else:
            for slot, maps in slots:
                at = pl.multiple_of(traced(maps, head, n_head) * width, width)
                pieces.append((at, in_ref[slot * rows : (slot + 1) * rows, :]))
            residual = pieces[0][1]
        square = None
        for _, piece in pieces:
            value = piece.astype(jnp.float32)
            square = value * value if square is None else square + value * value
        meansq = jnp.sum(square, axis=-1, keepdims=True) / feat
        inverse = lax.rsqrt(meansq + 1e-06)
        query = [None] * heads_dev
        fresh = [None] * heads_dev
        for at, piece in pieces:
            scale = 1.0 + scale_ref[:, pl.ds(at, width)]
            shift = shift_ref[:, pl.ds(at, width)]
            modded = (piece.astype(jnp.float32) * inverse * scale + shift).astype(jnp.bfloat16)
            for h in range(heads_dev):
                q = jnp.dot(modded, wq_ref[h, pl.ds(at, width), :], preferred_element_type=jnp.float32)
                kv = jnp.dot(modded, wkv_ref[h, pl.ds(at, width), :], preferred_element_type=jnp.float32)
                query[h] = q if query[h] is None else query[h] + q
                fresh[h] = kv if fresh[h] is None else fresh[h] + kv
        hidden = hidden_ref[...] != 0
        asking = lax.rem(lax.broadcasted_iota(jnp.int32, (rows, rows), 0), micro)
        asked = lax.rem(lax.broadcasted_iota(jnp.int32, (rows, rows), 1), micro)
        later = asked > asking
        score_scale = 1.0 / math.sqrt(head_dim)
        over_last = (((1,), (1,)), ((), ()))
        attended = []
        for h in range(heads_dev):
            q = query[h].astype(jnp.bfloat16)
            k = fresh[h][:, :head_dim].astype(jnp.bfloat16)
            v = fresh[h][:, head_dim:].astype(jnp.bfloat16)
            old = lax.dot_general(q, key_ref[h], over_last, preferred_element_type=jnp.float32)
            old = old.reshape(rows // 8, 8, positions) * score_scale
            old = jnp.where(hidden[None], MASKED, old).reshape(rows, positions)
            new = lax.dot_general(q, k, over_last, preferred_element_type=jnp.float32)
            new = jnp.where(later, MASKED, new * score_scale)
            top = jnp.maximum(
                jnp.max(old, axis=-1, keepdims=True), jnp.max(new, axis=-1, keepdims=True)
            )
            old = jnp.exp(old - top)
            new = jnp.exp(new - top)
            total = jnp.sum(old, axis=-1, keepdims=True) + jnp.sum(new, axis=-1, keepdims=True)
            summed = jnp.dot(
                old.astype(jnp.bfloat16), val_ref[h], preferred_element_type=jnp.float32
            ) + jnp.dot(new.astype(jnp.bfloat16), v, preferred_element_type=jnp.float32)
            attended.append(summed / total)
        gate = gate_ref[:, pl.ds(own, width)]
        result = residual.astype(jnp.float32) + gate * jnp.concatenate(attended, axis=1)
        if by_token:
            order_ref = refs[11]
            part = rows // n_head
            for slot, maps in slots:
                order_ref[traced(maps, head, n_head)] = result[slot * part : (slot + 1) * part, :]
            result = order_ref[...].reshape(rows, width)
        out_ref[...] = result.reshape(out_ref.shape).astype(out_ref.dtype)


def run_layer(step, slots, micro, constants, held, blocks, out_shape):
    rows, width = held.shape
    n_head = lax.axis_size("head")
    return pl.pallas_call(
        functools.partial(layer_kernel, step, slots, micro),
        out_shape=jax.ShapeDtypeStruct(out_shape, held.dtype),
        in_specs=[VMEM] * (len(constants) + 2),
        out_specs=VMEM,
        scratch_shapes=[pltpu.VMEM((n_head, rows // n_head, width), jnp.float32)],
        compiler_params=pltpu.CompilerParams(vmem_limit_bytes=LIMIT),
    )(*(pltpu.with_memory_space_constraint(array, pltpu.VMEM) for array in constants), held, blocks)


def plans(n_head):
    pair = (("swap", 0), ("swap", n_head // 2))
    rest = tuple(("swap", k) for k in [0] + list(range(n_head // 2 - 1, 0, -1)))
    return ((0, pair), (0, rest)), ((1, pair), (0, rest))


def whole_heads(
    patch_in, patch_start, mod_scale, mod_shift, res_gate, query_weight, kv_weight, stale_keys, stale_values
):
    n_head = lax.axis_size("head")
    n_pipe = lax.axis_size("pipe")
    micro, rows_dev, feat = patch_in.shape
    heads_dev, positions, head_dim = stale_keys.shape[1:]
    width = heads_dev * head_dim
    patch = rows_dev * n_head
    rows = micro * patch
    entry_plan, step_plan = plans(n_head)
    mine = jnp.transpose(patch_in, (1, 0, 2)).reshape(1, rows // n_head, feat)
    arrays = (mod_scale, mod_shift, res_gate, query_weight[0], kv_weight[0], stale_keys[0], stale_values[0])
    constants = load(patch_start, arrays, micro, patch, positions)
    value, offsets = exchange(mine, entry_plan)
    held = jnp.zeros((rows, width), jnp.bfloat16)
    for step in range(n_pipe):
        out_shape = held.shape if step + 1 < n_pipe else (n_head, rows // n_head, width)
        held = run_layer(step, distinct(offsets, n_head), micro, constants, held, value, out_shape)
        if step + 1 < n_pipe:
            value, offsets = exchange(held, step_plan)
    back = lax.all_to_all(held, "head", split_axis=0, concat_axis=0, tiled=True)
    back = jnp.transpose(back.reshape(n_head, rows_dev, micro, width), (2, 1, 0, 3))
    return back.reshape(1, micro, rows_dev, feat)


def shifted(value, axis, steps):
    count = lax.axis_size(axis)
    leading, last = (max(0, -steps), min(count, count - steps))
    return lax.ppermute(value, axis, [(source, source + steps) for source in range(leading, last)])


def modulate(rows, scale_row, shift_row):
    values = rows.astype(jnp.float32)
    meansq = jnp.mean(values * values, axis=-1, keepdims=True)
    normed = values * lax.rsqrt(meansq + 1e-06)
    return (normed * (1.0 + scale_row) + shift_row).astype(jnp.bfloat16)


def feature_layout(modded, groups, splits):
    rows_dev, feat = modded.shape
    width = feat // splits
    pieces = jnp.transpose(modded.reshape(rows_dev, splits, width), (1, 0, 2))
    copies = jnp.broadcast_to(pieces[None], (groups, splits, rows_dev, width))
    return copies.reshape(groups * splits, rows_dev, width)


def project_partial(received, w_both):
    n_src, rows_dev, width = received.shape
    inputs = received.reshape(n_src * rows_dev, width)
    partial_sum = jnp.einsum("pf,hfe->phe", inputs, w_both, preferred_element_type=jnp.float32)
    return partial_sum.reshape(n_src, rows_dev, -1)


def sum_partials(returned, groups, splits, heads_dev):
    n_src, rows_dev, width = returned.shape
    triple = width // heads_dev
    summed = jnp.sum(returned.reshape(groups, splits, rows_dev, heads_dev, triple), axis=1)
    ordered = jnp.transpose(summed, (1, 0, 2, 3))
    return ordered.reshape(rows_dev, groups * heads_dev, triple).astype(jnp.bfloat16)


def head_layout(qkv_own, groups, splits):
    rows_dev, heads_all, triple = qkv_own.shape
    width = heads_all // groups * triple
    grouped = jnp.transpose(qkv_own.reshape(rows_dev, groups, width), (1, 0, 2))
    copies = jnp.broadcast_to(grouped[:, None], (groups, splits, rows_dev, width))
    return copies.reshape(groups * splits, rows_dev, width)


def attend_block(query_blk, keys_buf, vals_buf):
    score_scale = 1.0 / math.sqrt(query_blk.shape[-1])
    logit_scores = (
        jnp.einsum("qhd,hkd->hqk", query_blk, keys_buf, preferred_element_type=jnp.float32)
        * score_scale
    )
    top = jnp.max(logit_scores, axis=-1)
    expo = jnp.exp(logit_scores - top[..., None])
    total = jnp.sum(expo, axis=-1)
    softmax_weight = expo.astype(jnp.bfloat16)
    blended_values = jnp.einsum(
        "hqk,hkd->qhd", softmax_weight, vals_buf, preferred_element_type=jnp.float32
    )
    partial_out = blended_values / jnp.transpose(total)[..., None]
    return (partial_out, jnp.transpose(top), jnp.transpose(total))


def segment_attend(received, offset, keys_buf, vals_buf, key_base):
    heads_dev, shard_keys, head_dim = keys_buf.shape
    patch = received.shape[0] * received.shape[1]
    triples = received.reshape(patch, heads_dev, 3 * head_dim)
    query = triples[..., :head_dim]
    fresh = triples[..., head_dim:]
    position = key_base + jnp.arange(shard_keys, dtype=jnp.int32)
    relative = position - offset
    inside = ((relative >= 0) & (relative < patch))[None, :, None]
    picked = jnp.clip(relative, 0, patch - 1)
    taken = jnp.transpose(jnp.take(fresh, picked, axis=0), (1, 0, 2))
    new_keys = jnp.where(inside, taken[..., :head_dim], keys_buf)
    new_vals = jnp.where(inside, taken[..., head_dim:], vals_buf)
    block = min(512, patch)
    blocks = query.reshape(patch // block, block, heads_dev, head_dim)
    outs, tops, totals = lax.map(lambda blk: attend_block(blk, new_keys, new_vals), blocks)
    return (
        new_keys,
        new_vals,
        outs.reshape(patch, heads_dev, head_dim),
        tops.reshape(patch, heads_dev),
        totals.reshape(patch, heads_dev),
    )


def merge_parts(outs, tops, totals, groups, splits):
    n_dev, rows_dev, width = outs.shape
    heads_dev = tops.shape[-1]
    head_dim = width // heads_dev
    outs = outs.reshape(groups, splits, rows_dev, heads_dev, head_dim)
    tops = tops.reshape(groups, splits, rows_dev, heads_dev)
    totals = totals.reshape(groups, splits, rows_dev, heads_dev)
    peak = jnp.max(tops, axis=1, keepdims=True)
    weight = jnp.exp(tops - peak) * totals
    summed = jnp.sum(weight[..., None] * outs, axis=1) / jnp.sum(weight, axis=1)[..., None]
    return jnp.transpose(summed, (1, 0, 2, 3)).reshape(rows_dev, groups * width)


def per_device(
    patch_in,
    patch_start,
    mod_scale,
    mod_shift,
    res_gate,
    query_weight,
    kv_weight,
    stale_keys,
    stale_values,
):
    n_head = lax.axis_size("head")
    n_pipe = lax.axis_size("pipe")
    micro, rows_dev, feat = patch_in.shape
    heads_dev = stale_keys.shape[1]
    shard_keys = stale_keys.shape[2]
    head_dim = stale_keys.shape[3]
    splits = max(n_head // HEADS, 1)
    groups = n_head // splits
    patch = rows_dev * n_head
    head_index = lax.axis_index("head")
    segment = lax.axis_index("pipe")
    key_base = head_index % splits * shard_keys
    w_both = jnp.concatenate([query_weight[0], kv_weight[0]], axis=-1)
    scale_row = mod_scale[0]
    shift_row = mod_shift[0]
    gate_row = res_gate[0]

    def run_attention(valid, received, offset, keys_buf, vals_buf):

        def active(operands):
            return segment_attend(operands[0], operands[1], operands[2], operands[3], key_base)

        def resting(operands):
            return (
                operands[2],
                operands[3],
                jnp.zeros((patch, heads_dev, head_dim), jnp.float32),
                jnp.zeros((patch, heads_dev), jnp.float32),
                jnp.ones((patch, heads_dev), jnp.float32),
            )

        return lax.cond(valid, active, resting, (received, offset, keys_buf, vals_buf))

    def write_out(outputs, valid, index, updated):
        old = lax.dynamic_index_in_dim(outputs, index, 0, keepdims=False)
        return lax.dynamic_update_index_in_dim(outputs, jnp.where(valid, updated, old), index, 0)

    def entering(index, incoming):
        first = lax.dynamic_index_in_dim(patch_in, index, 0, keepdims=False)
        return jnp.where(segment == 0, first, incoming)

    outputs = jnp.zeros((micro, rows_dev, feat), jnp.bfloat16)
    incoming = jnp.zeros((rows_dev, feat), jnp.bfloat16)
    keys_buf = stale_keys[0]
    vals_buf = stale_values[0]

    def apart_step(step, carry):
        keys_buf, vals_buf, incoming, outputs = carry
        index = step - segment
        valid = (index >= 0) & (index < micro)
        safe = jnp.clip(index, 0, micro - 1)
        current = entering(safe, incoming)
        modded = modulate(current, scale_row, shift_row)
        recv_feat = lax.all_to_all(
            feature_layout(modded, groups, splits), "head", split_axis=0, concat_axis=0, tiled=True
        )
        partial_sum = project_partial(recv_feat, w_both)
        returned = lax.all_to_all(partial_sum, "head", split_axis=0, concat_axis=0, tiled=True)
        qkv_own = sum_partials(returned, groups, splits, heads_dev)
        recv_qkv = lax.all_to_all(
            head_layout(qkv_own, groups, splits), "head", split_axis=0, concat_axis=0, tiled=True
        )
        keys_buf, vals_buf, part_out, tops, totals = run_attention(
            valid, recv_qkv, patch_start[safe], keys_buf, vals_buf
        )
        outs_back, tops_back, totals_back = (
            lax.all_to_all(
                part_out.reshape(n_head, rows_dev, heads_dev * head_dim),
                "head",
                split_axis=0,
                concat_axis=0,
                tiled=True,
            ),
            lax.all_to_all(
                tops.reshape(n_head, rows_dev, heads_dev),
                "head",
                split_axis=0,
                concat_axis=0,
                tiled=True,
            ),
            lax.all_to_all(
                totals.reshape(n_head, rows_dev, heads_dev),
                "head",
                split_axis=0,
                concat_axis=0,
                tiled=True,
            ),
        )
        blended_values = merge_parts(outs_back, tops_back, totals_back, groups, splits)
        updated = (current.astype(jnp.float32) + gate_row * blended_values).astype(jnp.bfloat16)
        outputs = write_out(outputs, valid, safe, updated)
        incoming = shifted(updated, "pipe", 1)
        return (keys_buf, vals_buf, incoming, outputs)

    final = lax.fori_loop(
        0, micro + n_pipe - 1, apart_step, (keys_buf, vals_buf, incoming, outputs)
    )
    outputs = final[3]
    return outputs[None]


def solution(mesh):
    n_head = mesh.shape["head"]
    whole = n_head <= HEADS and n_head & (n_head - 1) == 0
    placed = (
        P(None, "head", None),
        P(),
        P("pipe", None),
        P("pipe", None),
        P("pipe", None),
        P("pipe", "head", None, None),
        P("pipe", "head", None, None),
        P("pipe", "head", None, None),
        P("pipe", "head", None, None),
    )
    return jax.shard_map(
        whole_heads if whole else per_device,
        mesh=mesh,
        in_specs=placed,
        out_specs=P("pipe", None, "head", None),
        check_vma=False,
    )
```

```python
import functools
import math

import jax
import jax.numpy as jnp
from jax import lax
from jax.experimental import pallas as pl
from jax.experimental.pallas import tpu as pltpu
from jax.sharding import PartitionSpec as P

HEADS = 16
MASKED = -3.0e38
LIMIT = 4 * 1024 * 1024
SMEM = pl.BlockSpec(memory_space=pltpu.SMEM)
VMEM = pl.BlockSpec(memory_space=pltpu.VMEM)
ANY = pl.BlockSpec(memory_space=pl.ANY)


def origin(head, kind, amount, count):
    if kind == "turn":
        return (head - amount + count) % count
    if kind == "ring":
        half = count // 2
        place = head // 2 + (head % 2) * (count - 1 - 2 * (head // 2))
        place = (place - amount + count) % count
        outer = place // half
        return 2 * (place + outer * (count - 1 - 2 * place)) + outer
    return head ^ amount


def traced(maps, head, count):
    for kind, amount in maps:
        head = origin(head, kind, amount, count)
    return head


def distinct(offsets, count):
    slots = {}
    for slot, maps in enumerate(offsets):
        slots.setdefault(tuple(traced(maps, head, count) for head in range(count)), (slot, maps))
    own = tuple(range(count))
    return [slots[own]] + [slots[key] for key in slots if key != own]


def routed(value, kind, amount, shift, stage, turn):
    n_pipe, n_head = lax.axis_size("pipe"), lax.axis_size("head")
    target = (stage + shift) % n_pipe
    onto = {p: (p + shift) % n_pipe for p in range(n_pipe)}
    if shift and turn > 1 and n_pipe % 2 == 0:
        rest = [p for p in range(n_pipe) if p not in (stage, target)]
        onto = {stage: target, target: stage}
        for first, second in zip(rest[::2], rest[1::2]):
            onto[first], onto[second] = second, first
    pairs = []
    for p in range(n_pipe):
        for h in range(n_head):
            if p == stage:
                source = origin(h, kind, amount, n_head)
            else:
                source = h if shift else origin(h, "swap", 1, n_head)
            pairs.append((p * n_head + source, onto[p] * n_head + h))
    return lax.ppermute(value, ("pipe", "head"), pairs)


def exchange(value, plan, stage, own=None, offsets=((),)):
    own = value if own is None else own
    for shift, moves in plan:
        parts, known, turn = [], [], 0
        for kind, amount in moves:
            if kind == "keep":
                parts.append(own)
                known += offsets
            else:
                parts.append(routed(value, kind, amount, shift, stage, turn))
                known += [((kind, amount),) + maps for maps in offsets]
                turn += 1
        value, offsets = jnp.concatenate(parts, 0), known
        own = value
        stage = (stage + shift) % lax.axis_size("pipe")
    return value, offsets


def copied(pairs, sems):
    copies = [
        pltpu.make_async_copy(source, result, sems.at[index])
        for index, (source, result) in enumerate(pairs)
    ]
    for copy in copies:
        copy.start()
    return copies


def weight_kernel(scale_in, shift_in, gate_in, wq_in, wkv_in, own_in, *refs):
    scale_ref, shift_ref, gate_ref, weight_ref, own_ref, sems = refs
    heads_dev, _, head_dim = wq_in.shape
    width = heads_dev * head_dim
    pairs = [(own_in, own_ref)]
    for h in range(heads_dev):
        begin = h * head_dim
        pairs.append((wq_in.at[h], weight_ref.at[:, begin : begin + head_dim]))
        for part in range(2):
            begin += width
            source = wkv_in.at[h, :, part * head_dim : (part + 1) * head_dim]
            pairs.append((source, weight_ref.at[:, begin : begin + head_dim]))
    pairs += [(scale_in, scale_ref), (shift_in, shift_ref), (gate_in, gate_ref)]
    for copy in copied(pairs, sems):
        copy.wait()


def cache_kernel(micro, patch, start_in, key_in, val_in, after_ref, *refs):
    key_ref, val_ref, hidden_ref, start_ref, sems = refs
    heads_dev, _, head_dim = key_in.shape
    pairs = [(start_in, start_ref)]
    for h in range(heads_dev):
        lanes = slice(h * head_dim, (h + 1) * head_dim)
        pairs.append((key_in.at[h], key_ref.at[:, lanes]))
        pairs.append((val_in.at[h], val_ref.at[:, lanes]))
    copies = copied(pairs, sems)
    copies[0].wait()
    position = lax.broadcasted_iota(jnp.int32, hidden_ref.shape, 1)
    patch_row = lax.rem(lax.broadcasted_iota(jnp.int32, hidden_ref.shape, 0), micro)
    hidden = jnp.zeros(hidden_ref.shape, jnp.int32)
    for m in range(micro):
        relative = position - start_ref[m]
        inside = (relative >= 0) & (relative < patch) & (patch_row >= m)
        hidden = jnp.where(inside, 1, hidden)
    hidden_ref[...] = hidden
    for copy in copies[1:]:
        copy.wait()


def loaded(kernel, arrays, shapes, scratch, copies, cost, after=()):
    return pl.pallas_call(
        kernel,
        out_shape=[pltpu.VMEM(shape, dtype) for shape, dtype in shapes],
        in_specs=[ANY] * (len(arrays) + len(after)),
        out_specs=[VMEM] * len(shapes),
        scratch_shapes=scratch + [pltpu.SemaphoreType.DMA((copies,))],
        compiler_params=pltpu.CompilerParams(vmem_limit_bytes=LIMIT),
        cost_estimate=pl.CostEstimate(flops=0, bytes_accessed=cost, transcendentals=0),
    )(*(pltpu.with_memory_space_constraint(array, pltpu.HBM) for array in arrays), *after)


def layer_kernel(step, slots, micro, head_dim, *refs):
    scale_ref, shift_ref, gate_ref, weight_ref, key_ref, val_ref, hidden_ref, held_ref, in_ref, out_ref = refs[:10]
    stage = lax.axis_index("pipe")
    head = lax.axis_index("head")
    n_head = lax.axis_size("head")
    feat, positions = weight_ref.shape[0], key_ref.shape[0]
    rows, width = held_ref.shape
    heads_dev = width // head_dim
    by_token = len(in_ref.shape) == 3
    own = pl.multiple_of(head * width, width)

    @pl.when(stage != step)
    def _():
        out_ref[...] = held_ref[...].reshape(out_ref.shape)

    @pl.when(stage == step)
    def _():
        pieces = []
        if by_token:
            for index in range(n_head):
                at = index * width
                pieces.append((at, in_ref[:, :, at : at + width].astype(jnp.float32).reshape(rows, width)))
            residual = in_ref[:, :, pl.ds(own, width)].astype(jnp.float32).reshape(rows, width)
        else:
            for slot, maps in slots:
                at = pl.multiple_of(traced(maps, head, n_head) * width, width)
                pieces.append((at, in_ref[slot * rows : (slot + 1) * rows, :]))
            residual = pieces[0][1]
        square = None
        for _, piece in pieces:
            value = piece.astype(jnp.float32)
            square = value * value if square is None else square + value * value
        meansq = jnp.sum(square, axis=-1, keepdims=True) / feat
        inverse = lax.rsqrt(meansq + 1e-06)
        projected = None
        for at, piece in pieces:
            scale = 1.0 + scale_ref[:, pl.ds(at, width)]
            shift = shift_ref[:, pl.ds(at, width)]
            modded = (piece.astype(jnp.float32) * inverse * scale + shift).astype(jnp.bfloat16)
            term = jnp.dot(modded, weight_ref[pl.ds(at, width), :], preferred_element_type=jnp.float32)
            projected = term if projected is None else projected + term
        projected = projected.astype(jnp.bfloat16)
        query, fresh_keys, fresh_vals = (projected[:, part * width : (part + 1) * width] for part in range(3))
        lane_head = lax.broadcasted_iota(jnp.int32, (rows, width), 1) // head_dim
        queries = jnp.concatenate(
            [jnp.where(lane_head == h, query, jnp.zeros_like(query)) for h in range(heads_dev)], axis=0
        )
        asked_rows = heads_dev * rows
        hidden = hidden_ref[...] != 0
        asking = lax.rem(lax.broadcasted_iota(jnp.int32, (asked_rows, rows), 0), micro)
        asked = lax.rem(lax.broadcasted_iota(jnp.int32, (asked_rows, rows), 1), micro)
        later = asked > asking
        score_scale = 1.0 / math.sqrt(head_dim)
        over_last = (((1,), (1,)), ((), ()))
        old = lax.dot_general(queries, key_ref[...], over_last, preferred_element_type=jnp.float32)
        old = old.reshape(asked_rows // 8, 8, positions) * score_scale
        old = jnp.where(hidden[None], MASKED, old).reshape(asked_rows, positions)
        new = lax.dot_general(queries, fresh_keys, over_last, preferred_element_type=jnp.float32)
        new = jnp.where(later, MASKED, new * score_scale)
        top = jnp.maximum(jnp.max(old, axis=-1, keepdims=True), jnp.max(new, axis=-1, keepdims=True))
        old = jnp.exp(old - top)
        new = jnp.exp(new - top)
        total = jnp.sum(old, axis=-1, keepdims=True) + jnp.sum(new, axis=-1, keepdims=True)
        summed = jnp.dot(
            old.astype(jnp.bfloat16), val_ref[...], preferred_element_type=jnp.float32
        ) + jnp.dot(new.astype(jnp.bfloat16), fresh_vals, preferred_element_type=jnp.float32)
        averaged = summed / total
        attended = [
            averaged[h * rows : (h + 1) * rows, h * head_dim : (h + 1) * head_dim] for h in range(heads_dev)
        ]
        gate = gate_ref[:, pl.ds(own, width)]
        result = residual.astype(jnp.float32) + gate * jnp.concatenate(attended, axis=1)
        if by_token:
            order_ref = refs[10]
            part = rows // n_head
            for slot, maps in slots:
                order_ref[traced(maps, head, n_head)] = result[slot * part : (slot + 1) * part, :]
            result = order_ref[...].reshape(rows, width)
        out_ref[...] = result.reshape(out_ref.shape).astype(out_ref.dtype)


def run_layer(step, slots, micro, head_dim, constants, held, blocks, out_shape):
    rows, width = held.shape
    n_head = lax.axis_size("head")
    return pl.pallas_call(
        functools.partial(layer_kernel, step, slots, micro, head_dim),
        out_shape=jax.ShapeDtypeStruct(out_shape, held.dtype),
        in_specs=[VMEM] * (len(constants) + 2),
        out_specs=VMEM,
        scratch_shapes=[pltpu.VMEM((n_head, rows // n_head, width), jnp.float32)],
        compiler_params=pltpu.CompilerParams(vmem_limit_bytes=LIMIT),
    )(*(pltpu.with_memory_space_constraint(array, pltpu.VMEM) for array in constants), held, blocks)


def plans(n_head):
    keep = ("keep", 0)
    far = tuple(("swap", k) for k in range(n_head - 2, 0, -2))
    entry = ((1, (keep,) + far), (0, (keep, ("swap", 1))))
    return entry, ((1, tuple(("swap", k) for k in range(n_head - 1, -1, -1))),)


def whole_heads(
    patch_in, patch_start, mod_scale, mod_shift, res_gate, query_weight, kv_weight, stale_keys, stale_values
):
    n_head = lax.axis_size("head")
    n_pipe = lax.axis_size("pipe")
    micro, rows_dev, feat = patch_in.shape
    heads_dev, head_dim = stale_keys.shape[1], stale_keys.shape[3]
    width = heads_dev * head_dim
    patch = rows_dev * n_head
    rows = micro * patch
    entry_plan, step_plan = plans(n_head)
    mine = jnp.transpose(patch_in, (1, 0, 2)).reshape(1, rows // n_head, feat)
    positions = stale_keys.shape[2]
    row, half = (mod_scale.shape, mod_scale.dtype), jnp.bfloat16
    *params, own = loaded(
        weight_kernel,
        (mod_scale, mod_shift, res_gate, query_weight[0], kv_weight[0], mine),
        [row] * 3 + [((feat, 3 * width), half), (mine.shape, half)],
        [],
        4 + 3 * heads_dev,
        6 * feat * 3 * width,
    )
    value, offsets = exchange(mine, entry_plan[:1], n_pipe - 1, own)
    caches = loaded(
        functools.partial(cache_kernel, micro, patch),
        (patch_start, stale_keys[0], stale_values[0]),
        [((positions, width), half)] * 2 + [((8, positions), jnp.int32)],
        [pltpu.SMEM(patch_start.shape, patch_start.dtype)],
        1 + 2 * heads_dev,
        6 * positions * 2 * width,
        (value,),
    )
    value, offsets = exchange(value, entry_plan[1:], 0, offsets=offsets)
    constants = (*params, *caches)
    held = jnp.zeros((rows, width), jnp.bfloat16)
    for step in range(n_pipe):
        out_shape = held.shape if step + 1 < n_pipe else (n_head, rows // n_head, width)
        held = run_layer(step, distinct(offsets, n_head), micro, head_dim, constants, held, value, out_shape)
        if step + 1 < n_pipe:
            value, offsets = exchange(held, step_plan, step)
    back = lax.all_to_all(held, "head", split_axis=0, concat_axis=0, tiled=True)
    back = jnp.transpose(back.reshape(n_head, rows_dev, micro, width), (2, 1, 0, 3))
    return back.reshape(1, micro, rows_dev, feat)


def shifted(value, axis, steps):
    count = lax.axis_size(axis)
    leading, last = (max(0, -steps), min(count, count - steps))
    return lax.ppermute(value, axis, [(source, source + steps) for source in range(leading, last)])


def modulate(rows, scale_row, shift_row):
    values = rows.astype(jnp.float32)
    meansq = jnp.mean(values * values, axis=-1, keepdims=True)
    normed = values * lax.rsqrt(meansq + 1e-06)
    return (normed * (1.0 + scale_row) + shift_row).astype(jnp.bfloat16)


def feature_layout(modded, groups, splits):
    rows_dev, feat = modded.shape
    width = feat // splits
    pieces = jnp.transpose(modded.reshape(rows_dev, splits, width), (1, 0, 2))
    copies = jnp.broadcast_to(pieces[None], (groups, splits, rows_dev, width))
    return copies.reshape(groups * splits, rows_dev, width)


def project_partial(received, w_both):
    n_src, rows_dev, width = received.shape
    inputs = received.reshape(n_src * rows_dev, width)
    partial_sum = jnp.einsum("pf,hfe->phe", inputs, w_both, preferred_element_type=jnp.float32)
    return partial_sum.reshape(n_src, rows_dev, -1)


def sum_partials(returned, groups, splits, heads_dev):
    n_src, rows_dev, width = returned.shape
    triple = width // heads_dev
    summed = jnp.sum(returned.reshape(groups, splits, rows_dev, heads_dev, triple), axis=1)
    ordered = jnp.transpose(summed, (1, 0, 2, 3))
    return ordered.reshape(rows_dev, groups * heads_dev, triple).astype(jnp.bfloat16)


def head_layout(qkv_own, groups, splits):
    rows_dev, heads_all, triple = qkv_own.shape
    width = heads_all // groups * triple
    grouped = jnp.transpose(qkv_own.reshape(rows_dev, groups, width), (1, 0, 2))
    copies = jnp.broadcast_to(grouped[:, None], (groups, splits, rows_dev, width))
    return copies.reshape(groups * splits, rows_dev, width)


def attend_block(query_blk, keys_buf, vals_buf):
    score_scale = 1.0 / math.sqrt(query_blk.shape[-1])
    logit_scores = (
        jnp.einsum("qhd,hkd->hqk", query_blk, keys_buf, preferred_element_type=jnp.float32)
        * score_scale
    )
    top = jnp.max(logit_scores, axis=-1)
    expo = jnp.exp(logit_scores - top[..., None])
    total = jnp.sum(expo, axis=-1)
    softmax_weight = expo.astype(jnp.bfloat16)
    blended_values = jnp.einsum(
        "hqk,hkd->qhd", softmax_weight, vals_buf, preferred_element_type=jnp.float32
    )
    partial_out = blended_values / jnp.transpose(total)[..., None]
    return (partial_out, jnp.transpose(top), jnp.transpose(total))


def segment_attend(received, offset, keys_buf, vals_buf, key_base):
    heads_dev, shard_keys, head_dim = keys_buf.shape
    patch = received.shape[0] * received.shape[1]
    triples = received.reshape(patch, heads_dev, 3 * head_dim)
    query = triples[..., :head_dim]
    fresh = triples[..., head_dim:]
    position = key_base + jnp.arange(shard_keys, dtype=jnp.int32)
    relative = position - offset
    inside = ((relative >= 0) & (relative < patch))[None, :, None]
    picked = jnp.clip(relative, 0, patch - 1)
    taken = jnp.transpose(jnp.take(fresh, picked, axis=0), (1, 0, 2))
    new_keys = jnp.where(inside, taken[..., :head_dim], keys_buf)
    new_vals = jnp.where(inside, taken[..., head_dim:], vals_buf)
    block = min(512, patch)
    blocks = query.reshape(patch // block, block, heads_dev, head_dim)
    outs, tops, totals = lax.map(lambda blk: attend_block(blk, new_keys, new_vals), blocks)
    return (
        new_keys,
        new_vals,
        outs.reshape(patch, heads_dev, head_dim),
        tops.reshape(patch, heads_dev),
        totals.reshape(patch, heads_dev),
    )


def merge_parts(outs, tops, totals, groups, splits):
    n_dev, rows_dev, width = outs.shape
    heads_dev = tops.shape[-1]
    head_dim = width // heads_dev
    outs = outs.reshape(groups, splits, rows_dev, heads_dev, head_dim)
    tops = tops.reshape(groups, splits, rows_dev, heads_dev)
    totals = totals.reshape(groups, splits, rows_dev, heads_dev)
    peak = jnp.max(tops, axis=1, keepdims=True)
    weight = jnp.exp(tops - peak) * totals
    summed = jnp.sum(weight[..., None] * outs, axis=1) / jnp.sum(weight, axis=1)[..., None]
    return jnp.transpose(summed, (1, 0, 2, 3)).reshape(rows_dev, groups * width)


def per_device(
    patch_in,
    patch_start,
    mod_scale,
    mod_shift,
    res_gate,
    query_weight,
    kv_weight,
    stale_keys,
    stale_values,
):
    n_head = lax.axis_size("head")
    n_pipe = lax.axis_size("pipe")
    micro, rows_dev, feat = patch_in.shape
    heads_dev = stale_keys.shape[1]
    shard_keys = stale_keys.shape[2]
    head_dim = stale_keys.shape[3]
    splits = max(n_head // HEADS, 1)
    groups = n_head // splits
    patch = rows_dev * n_head
    head_index = lax.axis_index("head")
    segment = lax.axis_index("pipe")
    key_base = head_index % splits * shard_keys
    w_both = jnp.concatenate([query_weight[0], kv_weight[0]], axis=-1)
    scale_row = mod_scale[0]
    shift_row = mod_shift[0]
    gate_row = res_gate[0]

    def run_attention(valid, received, offset, keys_buf, vals_buf):

        def active(operands):
            return segment_attend(operands[0], operands[1], operands[2], operands[3], key_base)

        def resting(operands):
            return (
                operands[2],
                operands[3],
                jnp.zeros((patch, heads_dev, head_dim), jnp.float32),
                jnp.zeros((patch, heads_dev), jnp.float32),
                jnp.ones((patch, heads_dev), jnp.float32),
            )

        return lax.cond(valid, active, resting, (received, offset, keys_buf, vals_buf))

    def write_out(outputs, valid, index, updated):
        old = lax.dynamic_index_in_dim(outputs, index, 0, keepdims=False)
        return lax.dynamic_update_index_in_dim(outputs, jnp.where(valid, updated, old), index, 0)

    def entering(index, incoming):
        first = lax.dynamic_index_in_dim(patch_in, index, 0, keepdims=False)
        return jnp.where(segment == 0, first, incoming)

    outputs = jnp.zeros((micro, rows_dev, feat), jnp.bfloat16)
    incoming = jnp.zeros((rows_dev, feat), jnp.bfloat16)
    keys_buf = stale_keys[0]
    vals_buf = stale_values[0]

    def apart_step(step, carry):
        keys_buf, vals_buf, incoming, outputs = carry
        index = step - segment
        valid = (index >= 0) & (index < micro)
        safe = jnp.clip(index, 0, micro - 1)
        current = entering(safe, incoming)
        modded = modulate(current, scale_row, shift_row)
        recv_feat = lax.all_to_all(
            feature_layout(modded, groups, splits), "head", split_axis=0, concat_axis=0, tiled=True
        )
        partial_sum = project_partial(recv_feat, w_both)
        returned = lax.all_to_all(partial_sum, "head", split_axis=0, concat_axis=0, tiled=True)
        qkv_own = sum_partials(returned, groups, splits, heads_dev)
        recv_qkv = lax.all_to_all(
            head_layout(qkv_own, groups, splits), "head", split_axis=0, concat_axis=0, tiled=True
        )
        keys_buf, vals_buf, part_out, tops, totals = run_attention(
            valid, recv_qkv, patch_start[safe], keys_buf, vals_buf
        )
        outs_back, tops_back, totals_back = (
            lax.all_to_all(
                part_out.reshape(n_head, rows_dev, heads_dev * head_dim),
                "head",
                split_axis=0,
                concat_axis=0,
                tiled=True,
            ),
            lax.all_to_all(
                tops.reshape(n_head, rows_dev, heads_dev),
                "head",
                split_axis=0,
                concat_axis=0,
                tiled=True,
            ),
            lax.all_to_all(
                totals.reshape(n_head, rows_dev, heads_dev),
                "head",
                split_axis=0,
                concat_axis=0,
                tiled=True,
            ),
        )
        blended_values = merge_parts(outs_back, tops_back, totals_back, groups, splits)
        updated = (current.astype(jnp.float32) + gate_row * blended_values).astype(jnp.bfloat16)
        outputs = write_out(outputs, valid, safe, updated)
        incoming = shifted(updated, "pipe", 1)
        return (keys_buf, vals_buf, incoming, outputs)

    final = lax.fori_loop(
        0, micro + n_pipe - 1, apart_step, (keys_buf, vals_buf, incoming, outputs)
    )
    outputs = final[3]
    return outputs[None]


def solution(mesh):
    n_head = mesh.shape["head"]
    whole = n_head <= HEADS and n_head & (n_head - 1) == 0
    placed = (
        P(None, "head", None),
        P(),
        P("pipe", None),
        P("pipe", None),
        P("pipe", None),
        P("pipe", "head", None, None),
        P("pipe", "head", None, None),
        P("pipe", "head", None, None),
        P("pipe", "head", None, None),
    )
    return jax.shard_map(
        whole_heads if whole else per_device,
        mesh=mesh,
        in_specs=placed,
        out_specs=P("pipe", None, "head", None),
        check_vma=False,
    )
```

```python
import functools
import math

import jax
import jax.numpy as jnp
from jax import lax
from jax.experimental import pallas as pl
from jax.experimental.pallas import tpu as pltpu
from jax.sharding import PartitionSpec as P

HEADS = 16
MASKED = -3.0e38
LIMIT = 4 * 1024 * 1024
SMEM = pl.BlockSpec(memory_space=pltpu.SMEM)
VMEM = pl.BlockSpec(memory_space=pltpu.VMEM)
ANY = pl.BlockSpec(memory_space=pl.ANY)


def origin(head, kind, amount, count):
    if kind == "turn":
        return (head - amount + count) % count
    if kind == "ring":
        half = count // 2
        place = head // 2 + (head % 2) * (count - 1 - 2 * (head // 2))
        place = (place - amount + count) % count
        outer = place // half
        return 2 * (place + outer * (count - 1 - 2 * place)) + outer
    return head ^ amount


def traced(maps, head, count):
    for kind, amount in maps:
        head = origin(head, kind, amount, count)
    return head


def distinct(offsets, count):
    slots = {}
    for slot, maps in enumerate(offsets):
        slots.setdefault(tuple(traced(maps, head, count) for head in range(count)), (slot, maps))
    own = tuple(range(count))
    return [slots[own]] + [slots[key] for key in slots if key != own]


def routed(value, kind, amount, shift, stage, turn):
    n_pipe, n_head = lax.axis_size("pipe"), lax.axis_size("head")
    target = (stage + shift) % n_pipe
    onto = {p: (p + shift) % n_pipe for p in range(n_pipe)}
    if shift and turn > 1 and n_pipe % 2 == 0:
        rest = [p for p in range(n_pipe) if p not in (stage, target)]
        onto = {stage: target, target: stage}
        for first, second in zip(rest[::2], rest[1::2]):
            onto[first], onto[second] = second, first
    pairs = []
    for p in range(n_pipe):
        for h in range(n_head):
            if p == stage:
                source = origin(h, kind, amount, n_head)
            else:
                source = h if shift else origin(h, "swap", 1, n_head)
            pairs.append((p * n_head + source, onto[p] * n_head + h))
    return lax.ppermute(value, ("pipe", "head"), pairs)


def exchange(value, plan, stage, own=None, offsets=((),)):
    own = value if own is None else own
    for shift, moves in plan:
        parts, known, turn = [], [], 0
        for kind, amount in moves:
            if kind == "keep":
                parts.append(own)
                known += offsets
            else:
                parts.append(routed(value, kind, amount, shift, stage, turn))
                known += [((kind, amount),) + maps for maps in offsets]
                turn += 1
        value, offsets = jnp.concatenate(parts, 0), known
        own = value
        stage = (stage + shift) % lax.axis_size("pipe")
    return value, offsets


def copied(pairs, sems):
    copies = [
        pltpu.make_async_copy(source, result, sems.at[index])
        for index, (source, result) in enumerate(pairs)
    ]
    for copy in copies:
        copy.start()
    return copies


def weight_kernel(scale_in, shift_in, gate_in, wq_in, wkv_in, own_in, *refs):
    scale_ref, shift_ref, gate_ref, weight_ref, own_ref, sems = refs
    heads_dev, _, head_dim = wq_in.shape
    width = heads_dev * head_dim
    pairs = [(own_in, own_ref)]
    for h in range(heads_dev):
        begin = h * head_dim
        pairs.append((wq_in.at[h], weight_ref.at[:, begin : begin + head_dim]))
        for part in range(2):
            begin += width
            source = wkv_in.at[h, :, part * head_dim : (part + 1) * head_dim]
            pairs.append((source, weight_ref.at[:, begin : begin + head_dim]))
    pairs += [(scale_in, scale_ref), (shift_in, shift_ref), (gate_in, gate_ref)]
    for copy in copied(pairs, sems):
        copy.wait()


def cache_kernel(micro, patch, start_in, key_in, val_in, after_ref, *refs):
    key_ref, val_ref, hidden_ref, start_ref, sems = refs
    heads_dev, _, head_dim = key_in.shape
    pairs = [(start_in, start_ref)]
    for h in range(heads_dev):
        lanes = slice(h * head_dim, (h + 1) * head_dim)
        pairs.append((key_in.at[h], key_ref.at[:, lanes]))
        pairs.append((val_in.at[h], val_ref.at[:, lanes]))
    copies = copied(pairs, sems)
    copies[0].wait()
    position = lax.broadcasted_iota(jnp.int32, hidden_ref.shape, 1)
    patch_row = lax.rem(lax.broadcasted_iota(jnp.int32, hidden_ref.shape, 0), micro)
    hidden = jnp.zeros(hidden_ref.shape, jnp.int32)
    for m in range(micro):
        relative = position - start_ref[m]
        inside = (relative >= 0) & (relative < patch) & (patch_row >= m)
        hidden = jnp.where(inside, 1, hidden)
    hidden_ref[...] = hidden
    for copy in copies[1:]:
        copy.wait()


def loaded(kernel, arrays, shapes, scratch, copies, cost, after=()):
    return pl.pallas_call(
        kernel,
        out_shape=[pltpu.VMEM(shape, dtype) for shape, dtype in shapes],
        in_specs=[ANY] * (len(arrays) + len(after)),
        out_specs=[VMEM] * len(shapes),
        scratch_shapes=scratch + [pltpu.SemaphoreType.DMA((copies,))],
        compiler_params=pltpu.CompilerParams(vmem_limit_bytes=LIMIT),
        cost_estimate=pl.CostEstimate(flops=0, bytes_accessed=cost, transcendentals=0),
    )(*(pltpu.with_memory_space_constraint(array, pltpu.HBM) for array in arrays), *after)


def layer_kernel(step, slots, micro, head_dim, *refs):
    scale_ref, shift_ref, gate_ref, weight_ref, key_ref, val_ref, hidden_ref, held_ref, in_ref, out_ref = refs[:10]
    stage = lax.axis_index("pipe")
    head = lax.axis_index("head")
    n_head = lax.axis_size("head")
    feat, positions = weight_ref.shape[0], key_ref.shape[0]
    rows, width = held_ref.shape
    heads_dev = width // head_dim
    by_token = len(in_ref.shape) == 3
    own = pl.multiple_of(head * width, width)

    @pl.when(stage != step)
    def _():
        out_ref[...] = held_ref[...].reshape(out_ref.shape)

    @pl.when(stage == step)
    def _():
        pieces = []
        if by_token:
            for index in range(n_head):
                at = index * width
                pieces.append((at, in_ref[:, :, at : at + width].astype(jnp.float32).reshape(rows, width)))
            residual = in_ref[:, :, pl.ds(own, width)].astype(jnp.float32).reshape(rows, width)
        else:
            for slot, maps in slots:
                at = pl.multiple_of(traced(maps, head, n_head) * width, width)
                pieces.append((at, in_ref[slot * rows : (slot + 1) * rows, :]))
            residual = pieces[0][1]
        square, projected = None, None
        for at, piece in pieces:
            value = piece.astype(jnp.float32)
            square = value * value if square is None else square + value * value
            scaled = (value * (1.0 + scale_ref[:, pl.ds(at, width)])).astype(jnp.bfloat16)
            shift = shift_ref[:, pl.ds(at, width)].astype(jnp.bfloat16)
            both = jnp.concatenate([scaled, jnp.broadcast_to(shift, (16, width))], axis=0)
            term = jnp.dot(both, weight_ref[pl.ds(at, width), :], preferred_element_type=jnp.float32)
            projected = term if projected is None else projected + term
        inverse = lax.rsqrt(jnp.sum(square, axis=-1, keepdims=True) / feat + 1e-06)
        projected = (projected[:rows] * inverse + projected[rows : rows + 1]).astype(jnp.bfloat16)
        query, fresh_keys, fresh_vals = (projected[:, part * width : (part + 1) * width] for part in range(3))
        lane_head = lax.broadcasted_iota(jnp.int32, (rows, width), 1) // head_dim
        queries = jnp.concatenate(
            [jnp.where(lane_head == h, query, jnp.zeros_like(query)) for h in range(heads_dev)], axis=0
        )
        asked_rows = heads_dev * rows
        hidden = hidden_ref[...] != 0
        asking = lax.rem(lax.broadcasted_iota(jnp.int32, (asked_rows, rows), 0), micro)
        asked = lax.rem(lax.broadcasted_iota(jnp.int32, (asked_rows, rows), 1), micro)
        later = asked > asking
        score_scale = 1.0 / math.sqrt(head_dim)
        over_last = (((1,), (1,)), ((), ()))
        old = lax.dot_general(queries, key_ref[...], over_last, preferred_element_type=jnp.float32)
        old = old.reshape(asked_rows // 8, 8, positions) * score_scale
        old = jnp.where(hidden[None], MASKED, old).reshape(asked_rows, positions)
        new = lax.dot_general(queries, fresh_keys, over_last, preferred_element_type=jnp.float32)
        new = jnp.where(later, MASKED, new * score_scale)
        top = jnp.maximum(jnp.max(old, axis=-1, keepdims=True), jnp.max(new, axis=-1, keepdims=True))
        old = jnp.exp(old - top)
        new = jnp.exp(new - top)
        total = jnp.sum(old, axis=-1, keepdims=True) + jnp.sum(new, axis=-1, keepdims=True)
        summed = jnp.dot(
            old.astype(jnp.bfloat16), val_ref[...], preferred_element_type=jnp.float32
        ) + jnp.dot(new.astype(jnp.bfloat16), fresh_vals, preferred_element_type=jnp.float32)
        averaged = summed / total
        attended = [
            averaged[h * rows : (h + 1) * rows, h * head_dim : (h + 1) * head_dim] for h in range(heads_dev)
        ]
        gate = gate_ref[:, pl.ds(own, width)]
        result = residual.astype(jnp.float32) + gate * jnp.concatenate(attended, axis=1)
        if by_token:
            order_ref = refs[10]
            part = rows // n_head
            for slot, maps in slots:
                order_ref[traced(maps, head, n_head)] = result[slot * part : (slot + 1) * part, :]
            result = order_ref[...].reshape(rows, width)
        out_ref[...] = result.reshape(out_ref.shape).astype(out_ref.dtype)


def run_layer(step, slots, micro, head_dim, constants, held, blocks, out_shape):
    rows, width = held.shape
    n_head = lax.axis_size("head")
    return pl.pallas_call(
        functools.partial(layer_kernel, step, slots, micro, head_dim),
        out_shape=jax.ShapeDtypeStruct(out_shape, held.dtype),
        in_specs=[VMEM] * (len(constants) + 2),
        out_specs=VMEM,
        scratch_shapes=[pltpu.VMEM((n_head, rows // n_head, width), jnp.float32)],
        compiler_params=pltpu.CompilerParams(vmem_limit_bytes=LIMIT),
    )(*(pltpu.with_memory_space_constraint(array, pltpu.VMEM) for array in constants), held, blocks)


def plans(n_head):
    keep = ("keep", 0)
    far = tuple(("swap", k) for k in range(n_head - 2, 0, -2))
    entry = ((-1, (keep,) + far), (0, (keep, ("swap", 1))))
    return entry, ((1, tuple(("swap", k) for k in range(n_head - 1, -1, -1))),)


def whole_heads(
    patch_in, patch_start, mod_scale, mod_shift, res_gate, query_weight, kv_weight, stale_keys, stale_values
):
    n_head = lax.axis_size("head")
    n_pipe = lax.axis_size("pipe")
    micro, rows_dev, feat = patch_in.shape
    heads_dev, head_dim = stale_keys.shape[1], stale_keys.shape[3]
    width = heads_dev * head_dim
    patch = rows_dev * n_head
    rows = micro * patch
    entry_plan, step_plan = plans(n_head)
    mine = jnp.transpose(patch_in, (1, 0, 2)).reshape(1, rows // n_head, feat)
    positions = stale_keys.shape[2]
    row, half = (mod_scale.shape, mod_scale.dtype), jnp.bfloat16
    *params, own = loaded(
        weight_kernel,
        (mod_scale, mod_shift, res_gate, query_weight[0], kv_weight[0], mine),
        [row] * 3 + [((feat, 3 * width), half), (mine.shape, half)],
        [],
        4 + 3 * heads_dev,
        6 * feat * 3 * width,
    )
    value, offsets = exchange(mine, entry_plan[:1], 1, own)
    caches = loaded(
        functools.partial(cache_kernel, micro, patch),
        (patch_start, stale_keys[0], stale_values[0]),
        [((positions, width), half)] * 2 + [((8, positions), jnp.int32)],
        [pltpu.SMEM(patch_start.shape, patch_start.dtype)],
        1 + 2 * heads_dev,
        6 * positions * 2 * width,
        (value,),
    )
    value, offsets = exchange(value, entry_plan[1:], 0, offsets=offsets)
    constants = (*params, *caches)
    held = jnp.zeros((rows, width), jnp.bfloat16)
    for step in range(n_pipe):
        out_shape = held.shape if step + 1 < n_pipe else (n_head, rows // n_head, width)
        held = run_layer(step, distinct(offsets, n_head), micro, head_dim, constants, held, value, out_shape)
        if step + 1 < n_pipe:
            value, offsets = exchange(held, step_plan, step)
    back = lax.all_to_all(held, "head", split_axis=0, concat_axis=0, tiled=True)
    back = jnp.transpose(back.reshape(n_head, rows_dev, micro, width), (2, 1, 0, 3))
    return back.reshape(1, micro, rows_dev, feat)


def shifted(value, axis, steps):
    count = lax.axis_size(axis)
    leading, last = (max(0, -steps), min(count, count - steps))
    return lax.ppermute(value, axis, [(source, source + steps) for source in range(leading, last)])


def modulate(rows, scale_row, shift_row):
    values = rows.astype(jnp.float32)
    meansq = jnp.mean(values * values, axis=-1, keepdims=True)
    normed = values * lax.rsqrt(meansq + 1e-06)
    return (normed * (1.0 + scale_row) + shift_row).astype(jnp.bfloat16)


def feature_layout(modded, groups, splits):
    rows_dev, feat = modded.shape
    width = feat // splits
    pieces = jnp.transpose(modded.reshape(rows_dev, splits, width), (1, 0, 2))
    copies = jnp.broadcast_to(pieces[None], (groups, splits, rows_dev, width))
    return copies.reshape(groups * splits, rows_dev, width)


def project_partial(received, w_both):
    n_src, rows_dev, width = received.shape
    inputs = received.reshape(n_src * rows_dev, width)
    partial_sum = jnp.einsum("pf,hfe->phe", inputs, w_both, preferred_element_type=jnp.float32)
    return partial_sum.reshape(n_src, rows_dev, -1)


def sum_partials(returned, groups, splits, heads_dev):
    n_src, rows_dev, width = returned.shape
    triple = width // heads_dev
    summed = jnp.sum(returned.reshape(groups, splits, rows_dev, heads_dev, triple), axis=1)
    ordered = jnp.transpose(summed, (1, 0, 2, 3))
    return ordered.reshape(rows_dev, groups * heads_dev, triple).astype(jnp.bfloat16)


def head_layout(qkv_own, groups, splits):
    rows_dev, heads_all, triple = qkv_own.shape
    width = heads_all // groups * triple
    grouped = jnp.transpose(qkv_own.reshape(rows_dev, groups, width), (1, 0, 2))
    copies = jnp.broadcast_to(grouped[:, None], (groups, splits, rows_dev, width))
    return copies.reshape(groups * splits, rows_dev, width)


def attend_block(query_blk, keys_buf, vals_buf):
    score_scale = 1.0 / math.sqrt(query_blk.shape[-1])
    logit_scores = (
        jnp.einsum("qhd,hkd->hqk", query_blk, keys_buf, preferred_element_type=jnp.float32)
        * score_scale
    )
    top = jnp.max(logit_scores, axis=-1)
    expo = jnp.exp(logit_scores - top[..., None])
    total = jnp.sum(expo, axis=-1)
    softmax_weight = expo.astype(jnp.bfloat16)
    blended_values = jnp.einsum(
        "hqk,hkd->qhd", softmax_weight, vals_buf, preferred_element_type=jnp.float32
    )
    partial_out = blended_values / jnp.transpose(total)[..., None]
    return (partial_out, jnp.transpose(top), jnp.transpose(total))


def segment_attend(received, offset, keys_buf, vals_buf, key_base):
    heads_dev, shard_keys, head_dim = keys_buf.shape
    patch = received.shape[0] * received.shape[1]
    triples = received.reshape(patch, heads_dev, 3 * head_dim)
    query = triples[..., :head_dim]
    fresh = triples[..., head_dim:]
    position = key_base + jnp.arange(shard_keys, dtype=jnp.int32)
    relative = position - offset
    inside = ((relative >= 0) & (relative < patch))[None, :, None]
    picked = jnp.clip(relative, 0, patch - 1)
    taken = jnp.transpose(jnp.take(fresh, picked, axis=0), (1, 0, 2))
    new_keys = jnp.where(inside, taken[..., :head_dim], keys_buf)
    new_vals = jnp.where(inside, taken[..., head_dim:], vals_buf)
    block = min(512, patch)
    blocks = query.reshape(patch // block, block, heads_dev, head_dim)
    outs, tops, totals = lax.map(lambda blk: attend_block(blk, new_keys, new_vals), blocks)
    return (
        new_keys,
        new_vals,
        outs.reshape(patch, heads_dev, head_dim),
        tops.reshape(patch, heads_dev),
        totals.reshape(patch, heads_dev),
    )


def merge_parts(outs, tops, totals, groups, splits):
    n_dev, rows_dev, width = outs.shape
    heads_dev = tops.shape[-1]
    head_dim = width // heads_dev
    outs = outs.reshape(groups, splits, rows_dev, heads_dev, head_dim)
    tops = tops.reshape(groups, splits, rows_dev, heads_dev)
    totals = totals.reshape(groups, splits, rows_dev, heads_dev)
    peak = jnp.max(tops, axis=1, keepdims=True)
    weight = jnp.exp(tops - peak) * totals
    summed = jnp.sum(weight[..., None] * outs, axis=1) / jnp.sum(weight, axis=1)[..., None]
    return jnp.transpose(summed, (1, 0, 2, 3)).reshape(rows_dev, groups * width)


def per_device(
    patch_in,
    patch_start,
    mod_scale,
    mod_shift,
    res_gate,
    query_weight,
    kv_weight,
    stale_keys,
    stale_values,
):
    n_head = lax.axis_size("head")
    n_pipe = lax.axis_size("pipe")
    micro, rows_dev, feat = patch_in.shape
    heads_dev = stale_keys.shape[1]
    shard_keys = stale_keys.shape[2]
    head_dim = stale_keys.shape[3]
    splits = max(n_head // HEADS, 1)
    groups = n_head // splits
    patch = rows_dev * n_head
    head_index = lax.axis_index("head")
    segment = lax.axis_index("pipe")
    key_base = head_index % splits * shard_keys
    w_both = jnp.concatenate([query_weight[0], kv_weight[0]], axis=-1)
    scale_row = mod_scale[0]
    shift_row = mod_shift[0]
    gate_row = res_gate[0]

    def run_attention(valid, received, offset, keys_buf, vals_buf):

        def active(operands):
            return segment_attend(operands[0], operands[1], operands[2], operands[3], key_base)

        def resting(operands):
            return (
                operands[2],
                operands[3],
                jnp.zeros((patch, heads_dev, head_dim), jnp.float32),
                jnp.zeros((patch, heads_dev), jnp.float32),
                jnp.ones((patch, heads_dev), jnp.float32),
            )

        return lax.cond(valid, active, resting, (received, offset, keys_buf, vals_buf))

    def write_out(outputs, valid, index, updated):
        old = lax.dynamic_index_in_dim(outputs, index, 0, keepdims=False)
        return lax.dynamic_update_index_in_dim(outputs, jnp.where(valid, updated, old), index, 0)

    def entering(index, incoming):
        first = lax.dynamic_index_in_dim(patch_in, index, 0, keepdims=False)
        return jnp.where(segment == 0, first, incoming)

    outputs = jnp.zeros((micro, rows_dev, feat), jnp.bfloat16)
    incoming = jnp.zeros((rows_dev, feat), jnp.bfloat16)
    keys_buf = stale_keys[0]
    vals_buf = stale_values[0]

    def apart_step(step, carry):
        keys_buf, vals_buf, incoming, outputs = carry
        index = step - segment
        valid = (index >= 0) & (index < micro)
        safe = jnp.clip(index, 0, micro - 1)
        current = entering(safe, incoming)
        modded = modulate(current, scale_row, shift_row)
        recv_feat = lax.all_to_all(
            feature_layout(modded, groups, splits), "head", split_axis=0, concat_axis=0, tiled=True
        )
        partial_sum = project_partial(recv_feat, w_both)
        returned = lax.all_to_all(partial_sum, "head", split_axis=0, concat_axis=0, tiled=True)
        qkv_own = sum_partials(returned, groups, splits, heads_dev)
        recv_qkv = lax.all_to_all(
            head_layout(qkv_own, groups, splits), "head", split_axis=0, concat_axis=0, tiled=True
        )
        keys_buf, vals_buf, part_out, tops, totals = run_attention(
            valid, recv_qkv, patch_start[safe], keys_buf, vals_buf
        )
        outs_back, tops_back, totals_back = (
            lax.all_to_all(
                part_out.reshape(n_head, rows_dev, heads_dev * head_dim),
                "head",
                split_axis=0,
                concat_axis=0,
                tiled=True,
            ),
            lax.all_to_all(
                tops.reshape(n_head, rows_dev, heads_dev),
                "head",
                split_axis=0,
                concat_axis=0,
                tiled=True,
            ),
            lax.all_to_all(
                totals.reshape(n_head, rows_dev, heads_dev),
                "head",
                split_axis=0,
                concat_axis=0,
                tiled=True,
            ),
        )
        blended_values = merge_parts(outs_back, tops_back, totals_back, groups, splits)
        updated = (current.astype(jnp.float32) + gate_row * blended_values).astype(jnp.bfloat16)
        outputs = write_out(outputs, valid, safe, updated)
        incoming = shifted(updated, "pipe", 1)
        return (keys_buf, vals_buf, incoming, outputs)

    final = lax.fori_loop(
        0, micro + n_pipe - 1, apart_step, (keys_buf, vals_buf, incoming, outputs)
    )
    outputs = final[3]
    return outputs[None]


def solution(mesh):
    n_head = mesh.shape["head"]
    whole = n_head <= HEADS and n_head & (n_head - 1) == 0
    placed = (
        P(None, "head", None),
        P(),
        P("pipe", None),
        P("pipe", None),
        P("pipe", None),
        P("pipe", "head", None, None),
        P("pipe", "head", None, None),
        P("pipe", "head", None, None),
        P("pipe", "head", None, None),
    )
    return jax.shard_map(
        whole_heads if whole else per_device,
        mesh=mesh,
        in_specs=placed,
        out_specs=P("pipe", None, "head", None),
        check_vma=False,
    )
```

```python
import functools
import math

import jax
import jax.numpy as jnp
from jax import lax
from jax.experimental import pallas as pl
from jax.experimental.pallas import tpu as pltpu
from jax.sharding import PartitionSpec as P

HEADS = 16
MASKED = -3.0e38
LIMIT = 4 * 1024 * 1024
SMEM = pl.BlockSpec(memory_space=pltpu.SMEM)
VMEM = pl.BlockSpec(memory_space=pltpu.VMEM)
ANY = pl.BlockSpec(memory_space=pl.ANY)


def origin(head, kind, amount, count):
    if kind == "turn":
        return (head - amount + count) % count
    if kind == "ring":
        half = count // 2
        place = head // 2 + (head % 2) * (count - 1 - 2 * (head // 2))
        place = (place - amount + count) % count
        outer = place // half
        return 2 * (place + outer * (count - 1 - 2 * place)) + outer
    return head ^ amount


def traced(maps, head, count):
    for kind, amount in maps:
        head = origin(head, kind, amount, count)
    return head


def distinct(offsets, count):
    slots = {}
    for slot, maps in enumerate(offsets):
        slots.setdefault(tuple(traced(maps, head, count) for head in range(count)), (slot, maps))
    own = tuple(range(count))
    return [slots[own]] + [slots[key] for key in slots if key != own]


def routed(value, kind, amount, shift, stage, turn):
    n_pipe, n_head = lax.axis_size("pipe"), lax.axis_size("head")
    target = (stage + shift) % n_pipe
    onto = {p: (p + shift) % n_pipe for p in range(n_pipe)}
    if shift and turn > 1 and n_pipe % 2 == 0:
        rest = [p for p in range(n_pipe) if p not in (stage, target)]
        onto = {stage: target, target: stage}
        for first, second in zip(rest[::2], rest[1::2]):
            onto[first], onto[second] = second, first
    pairs = []
    for p in range(n_pipe):
        for h in range(n_head):
            if p == stage:
                source = origin(h, kind, amount, n_head)
            else:
                source = h if shift else origin(h, "swap", 1, n_head)
            pairs.append((p * n_head + source, onto[p] * n_head + h))
    return lax.ppermute(value, ("pipe", "head"), pairs)


def exchange(value, plan, stage, own=None, offsets=((),)):
    own = value if own is None else own
    for shift, moves in plan:
        parts, known, turn = [], [], 2 if shift < 0 else 0
        for kind, amount in moves:
            if kind == "keep":
                parts.append(own)
                known += offsets
            else:
                parts.append(routed(value, kind, amount, shift, stage, turn))
                known += [((kind, amount),) + maps for maps in offsets]
                turn += 1
        value, offsets = jnp.concatenate(parts, 0), known
        own = value
        stage = (stage + shift) % lax.axis_size("pipe")
    return value, offsets


def copied(pairs, sems):
    copies = [
        pltpu.make_async_copy(source, result, sems.at[index])
        for index, (source, result) in enumerate(pairs)
    ]
    for copy in copies:
        copy.start()
    return copies


def weight_kernel(scale_in, shift_in, gate_in, wq_in, wkv_in, own_in, *refs):
    scale_ref, shift_ref, gate_ref, weight_ref, own_ref, sems = refs
    heads_dev, _, head_dim = wq_in.shape
    width = heads_dev * head_dim
    pairs = [(own_in, own_ref)]
    for h in range(heads_dev):
        begin = h * head_dim
        pairs.append((wq_in.at[h], weight_ref.at[:, begin : begin + head_dim]))
        for part in range(2):
            begin += width
            source = wkv_in.at[h, :, part * head_dim : (part + 1) * head_dim]
            pairs.append((source, weight_ref.at[:, begin : begin + head_dim]))
    pairs += [(scale_in, scale_ref), (shift_in, shift_ref), (gate_in, gate_ref)]
    for copy in copied(pairs, sems):
        copy.wait()


def cache_kernel(micro, patch, start_in, key_in, val_in, after_ref, *refs):
    key_ref, val_ref, hidden_ref, start_ref, sems = refs
    heads_dev, _, head_dim = key_in.shape
    pairs = [(start_in, start_ref)]
    for h in range(heads_dev):
        lanes = slice(h * head_dim, (h + 1) * head_dim)
        pairs.append((key_in.at[h], key_ref.at[:, lanes]))
        pairs.append((val_in.at[h], val_ref.at[:, lanes]))
    copies = copied(pairs, sems)
    copies[0].wait()
    position = lax.broadcasted_iota(jnp.int32, hidden_ref.shape, 1)
    patch_row = lax.rem(lax.broadcasted_iota(jnp.int32, hidden_ref.shape, 0), micro)
    hidden = jnp.zeros(hidden_ref.shape, jnp.int32)
    for m in range(micro):
        relative = position - start_ref[m]
        inside = (relative >= 0) & (relative < patch) & (patch_row >= m)
        hidden = jnp.where(inside, 1, hidden)
    hidden_ref[...] = hidden
    for copy in copies[1:]:
        copy.wait()


def loaded(kernel, arrays, shapes, scratch, copies, cost, after=()):
    return pl.pallas_call(
        kernel,
        out_shape=[pltpu.VMEM(shape, dtype) for shape, dtype in shapes],
        in_specs=[ANY] * (len(arrays) + len(after)),
        out_specs=[VMEM] * len(shapes),
        scratch_shapes=scratch + [pltpu.SemaphoreType.DMA((copies,))],
        compiler_params=pltpu.CompilerParams(vmem_limit_bytes=LIMIT),
        cost_estimate=pl.CostEstimate(flops=0, bytes_accessed=cost, transcendentals=0),
    )(*(pltpu.with_memory_space_constraint(array, pltpu.HBM) for array in arrays), *after)


def layer_kernel(step, slots, micro, head_dim, *refs):
    scale_ref, shift_ref, gate_ref, weight_ref, key_ref, val_ref, hidden_ref, held_ref, in_ref, out_ref = refs[:10]
    stage = lax.axis_index("pipe")
    head = lax.axis_index("head")
    n_head = lax.axis_size("head")
    feat, positions = weight_ref.shape[0], key_ref.shape[0]
    rows, width = held_ref.shape
    heads_dev = width // head_dim
    by_token = len(in_ref.shape) == 3
    own = pl.multiple_of(head * width, width)

    @pl.when(stage != step)
    def _():
        out_ref[...] = held_ref[...].reshape(out_ref.shape)

    @pl.when(stage == step)
    def _():
        pieces = []
        if by_token:
            for index in range(n_head):
                at = index * width
                pieces.append((at, in_ref[:, :, at : at + width].astype(jnp.float32).reshape(rows, width)))
            residual = in_ref[:, :, pl.ds(own, width)].astype(jnp.float32).reshape(rows, width)
        else:
            for slot, maps in slots:
                at = pl.multiple_of(traced(maps, head, n_head) * width, width)
                pieces.append((at, in_ref[slot * rows : (slot + 1) * rows, :]))
            residual = pieces[0][1]
        square, projected = None, None
        for at, piece in pieces:
            value = piece.astype(jnp.float32)
            square = value * value if square is None else square + value * value
            scaled = (value * (1.0 + scale_ref[:, pl.ds(at, width)])).astype(jnp.bfloat16)
            shift = shift_ref[:, pl.ds(at, width)].astype(jnp.bfloat16)
            both = jnp.concatenate([scaled, jnp.broadcast_to(shift, (16, width))], axis=0)
            term = jnp.dot(both, weight_ref[pl.ds(at, width), :], preferred_element_type=jnp.float32)
            projected = term if projected is None else projected + term
        inverse = lax.rsqrt(jnp.sum(square, axis=-1, keepdims=True) / feat + 1e-06)
        projected = (projected[:rows] * inverse + projected[rows : rows + 1]).astype(jnp.bfloat16)
        query, fresh_keys, fresh_vals = (projected[:, part * width : (part + 1) * width] for part in range(3))
        lane_head = lax.broadcasted_iota(jnp.int32, (rows, width), 1) // head_dim
        queries = jnp.concatenate(
            [jnp.where(lane_head == h, query, jnp.zeros_like(query)) for h in range(heads_dev)], axis=0
        )
        asked_rows = heads_dev * rows
        hidden = hidden_ref[...] != 0
        asking = lax.rem(lax.broadcasted_iota(jnp.int32, (asked_rows, rows), 0), micro)
        asked = lax.rem(lax.broadcasted_iota(jnp.int32, (asked_rows, rows), 1), micro)
        later = asked > asking
        score_scale = 1.0 / math.sqrt(head_dim)
        over_last = (((1,), (1,)), ((), ()))
        old = lax.dot_general(queries, key_ref[...], over_last, preferred_element_type=jnp.float32)
        old = old.reshape(asked_rows // 8, 8, positions) * score_scale
        old = jnp.where(hidden[None], MASKED, old).reshape(asked_rows, positions)
        new = lax.dot_general(queries, fresh_keys, over_last, preferred_element_type=jnp.float32)
        new = jnp.where(later, MASKED, new * score_scale)
        top = jnp.maximum(jnp.max(old, axis=-1, keepdims=True), jnp.max(new, axis=-1, keepdims=True))
        old = jnp.exp(old - top)
        new = jnp.exp(new - top)
        total = jnp.sum(old, axis=-1, keepdims=True) + jnp.sum(new, axis=-1, keepdims=True)
        summed = jnp.dot(
            old.astype(jnp.bfloat16), val_ref[...], preferred_element_type=jnp.float32
        ) + jnp.dot(new.astype(jnp.bfloat16), fresh_vals, preferred_element_type=jnp.float32)
        averaged = summed / total
        attended = [
            averaged[h * rows : (h + 1) * rows, h * head_dim : (h + 1) * head_dim] for h in range(heads_dev)
        ]
        gate = gate_ref[:, pl.ds(own, width)]
        result = residual.astype(jnp.float32) + gate * jnp.concatenate(attended, axis=1)
        if by_token:
            order_ref = refs[10]
            part = rows // n_head
            for slot, maps in slots:
                order_ref[traced(maps, head, n_head)] = result[slot * part : (slot + 1) * part, :]
            result = order_ref[...].reshape(rows, width)
        out_ref[...] = result.reshape(out_ref.shape).astype(out_ref.dtype)


def run_layer(step, slots, micro, head_dim, constants, held, blocks, out_shape):
    rows, width = held.shape
    n_head = lax.axis_size("head")
    return pl.pallas_call(
        functools.partial(layer_kernel, step, slots, micro, head_dim),
        out_shape=jax.ShapeDtypeStruct(out_shape, held.dtype),
        in_specs=[VMEM] * (len(constants) + 2),
        out_specs=VMEM,
        scratch_shapes=[pltpu.VMEM((n_head, rows // n_head, width), jnp.float32)],
        compiler_params=pltpu.CompilerParams(vmem_limit_bytes=LIMIT),
    )(*(pltpu.with_memory_space_constraint(array, pltpu.VMEM) for array in constants), held, blocks)


def plans(n_head):
    keep = ("keep", 0)
    far = sorted(range(2, n_head, 2), key=lambda k: (k != n_head // 2, -k))
    far = tuple(("swap", k) for k in far)
    entry = ((0, (keep, ("swap", 1))), (-1, (keep,) + far))
    return entry, ((1, tuple(("swap", k) for k in range(n_head - 1, -1, -1))),)


def whole_heads(
    patch_in, patch_start, mod_scale, mod_shift, res_gate, query_weight, kv_weight, stale_keys, stale_values
):
    n_head = lax.axis_size("head")
    n_pipe = lax.axis_size("pipe")
    micro, rows_dev, feat = patch_in.shape
    heads_dev, head_dim = stale_keys.shape[1], stale_keys.shape[3]
    width = heads_dev * head_dim
    patch = rows_dev * n_head
    rows = micro * patch
    entry_plan, step_plan = plans(n_head)
    mine = jnp.transpose(patch_in, (1, 0, 2)).reshape(1, rows // n_head, feat)
    positions = stale_keys.shape[2]
    row, half = (mod_scale.shape, mod_scale.dtype), jnp.bfloat16
    *params, own = loaded(
        weight_kernel,
        (mod_scale, mod_shift, res_gate, query_weight[0], kv_weight[0], mine),
        [row] * 3 + [((feat, 3 * width), half), (mine.shape, half)],
        [],
        4 + 3 * heads_dev,
        6 * feat * 3 * width,
    )
    value, offsets = exchange(mine, entry_plan[:1], 1, own)
    caches = loaded(
        functools.partial(cache_kernel, micro, patch),
        (patch_start, stale_keys[0], stale_values[0]),
        [((positions, width), half)] * 2 + [((8, positions), jnp.int32)],
        [pltpu.SMEM(patch_start.shape, patch_start.dtype)],
        1 + 2 * heads_dev,
        6 * positions * 2 * width,
        (value,),
    )
    value, offsets = exchange(value, entry_plan[1:], 1, offsets=offsets)
    constants = (*params, *caches)
    held = jnp.zeros((rows, width), jnp.bfloat16)
    for step in range(n_pipe):
        out_shape = held.shape
        held = run_layer(step, distinct(offsets, n_head), micro, head_dim, constants, held, value, out_shape)
        if step + 1 < n_pipe:
            value, offsets = exchange(held, step_plan, step)
    back = lax.all_to_all(held, "head", split_axis=0, concat_axis=0, tiled=True)
    back = jnp.transpose(back.reshape(n_head, rows_dev, micro, width), (2, 1, 0, 3))
    return back.reshape(1, micro, rows_dev, feat)


def shifted(value, axis, steps):
    count = lax.axis_size(axis)
    leading, last = (max(0, -steps), min(count, count - steps))
    return lax.ppermute(value, axis, [(source, source + steps) for source in range(leading, last)])


def modulate(rows, scale_row, shift_row):
    values = rows.astype(jnp.float32)
    meansq = jnp.mean(values * values, axis=-1, keepdims=True)
    normed = values * lax.rsqrt(meansq + 1e-06)
    return (normed * (1.0 + scale_row) + shift_row).astype(jnp.bfloat16)


def feature_layout(modded, groups, splits):
    rows_dev, feat = modded.shape
    width = feat // splits
    pieces = jnp.transpose(modded.reshape(rows_dev, splits, width), (1, 0, 2))
    copies = jnp.broadcast_to(pieces[None], (groups, splits, rows_dev, width))
    return copies.reshape(groups * splits, rows_dev, width)


def project_partial(received, w_both):
    n_src, rows_dev, width = received.shape
    inputs = received.reshape(n_src * rows_dev, width)
    partial_sum = jnp.einsum("pf,hfe->phe", inputs, w_both, preferred_element_type=jnp.float32)
    return partial_sum.reshape(n_src, rows_dev, -1)


def sum_partials(returned, groups, splits, heads_dev):
    n_src, rows_dev, width = returned.shape
    triple = width // heads_dev
    summed = jnp.sum(returned.reshape(groups, splits, rows_dev, heads_dev, triple), axis=1)
    ordered = jnp.transpose(summed, (1, 0, 2, 3))
    return ordered.reshape(rows_dev, groups * heads_dev, triple).astype(jnp.bfloat16)


def head_layout(qkv_own, groups, splits):
    rows_dev, heads_all, triple = qkv_own.shape
    width = heads_all // groups * triple
    grouped = jnp.transpose(qkv_own.reshape(rows_dev, groups, width), (1, 0, 2))
    copies = jnp.broadcast_to(grouped[:, None], (groups, splits, rows_dev, width))
    return copies.reshape(groups * splits, rows_dev, width)


def attend_block(query_blk, keys_buf, vals_buf):
    score_scale = 1.0 / math.sqrt(query_blk.shape[-1])
    logit_scores = (
        jnp.einsum("qhd,hkd->hqk", query_blk, keys_buf, preferred_element_type=jnp.float32)
        * score_scale
    )
    top = jnp.max(logit_scores, axis=-1)
    expo = jnp.exp(logit_scores - top[..., None])
    total = jnp.sum(expo, axis=-1)
    softmax_weight = expo.astype(jnp.bfloat16)
    blended_values = jnp.einsum(
        "hqk,hkd->qhd", softmax_weight, vals_buf, preferred_element_type=jnp.float32
    )
    partial_out = blended_values / jnp.transpose(total)[..., None]
    return (partial_out, jnp.transpose(top), jnp.transpose(total))


def segment_attend(received, offset, keys_buf, vals_buf, key_base):
    heads_dev, shard_keys, head_dim = keys_buf.shape
    patch = received.shape[0] * received.shape[1]
    triples = received.reshape(patch, heads_dev, 3 * head_dim)
    query = triples[..., :head_dim]
    fresh = triples[..., head_dim:]
    position = key_base + jnp.arange(shard_keys, dtype=jnp.int32)
    relative = position - offset
    inside = ((relative >= 0) & (relative < patch))[None, :, None]
    picked = jnp.clip(relative, 0, patch - 1)
    taken = jnp.transpose(jnp.take(fresh, picked, axis=0), (1, 0, 2))
    new_keys = jnp.where(inside, taken[..., :head_dim], keys_buf)
    new_vals = jnp.where(inside, taken[..., head_dim:], vals_buf)
    block = min(512, patch)
    blocks = query.reshape(patch // block, block, heads_dev, head_dim)
    outs, tops, totals = lax.map(lambda blk: attend_block(blk, new_keys, new_vals), blocks)
    return (
        new_keys,
        new_vals,
        outs.reshape(patch, heads_dev, head_dim),
        tops.reshape(patch, heads_dev),
        totals.reshape(patch, heads_dev),
    )


def merge_parts(outs, tops, totals, groups, splits):
    n_dev, rows_dev, width = outs.shape
    heads_dev = tops.shape[-1]
    head_dim = width // heads_dev
    outs = outs.reshape(groups, splits, rows_dev, heads_dev, head_dim)
    tops = tops.reshape(groups, splits, rows_dev, heads_dev)
    totals = totals.reshape(groups, splits, rows_dev, heads_dev)
    peak = jnp.max(tops, axis=1, keepdims=True)
    weight = jnp.exp(tops - peak) * totals
    summed = jnp.sum(weight[..., None] * outs, axis=1) / jnp.sum(weight, axis=1)[..., None]
    return jnp.transpose(summed, (1, 0, 2, 3)).reshape(rows_dev, groups * width)


def per_device(
    patch_in,
    patch_start,
    mod_scale,
    mod_shift,
    res_gate,
    query_weight,
    kv_weight,
    stale_keys,
    stale_values,
):
    n_head = lax.axis_size("head")
    n_pipe = lax.axis_size("pipe")
    micro, rows_dev, feat = patch_in.shape
    heads_dev = stale_keys.shape[1]
    shard_keys = stale_keys.shape[2]
    head_dim = stale_keys.shape[3]
    splits = max(n_head // HEADS, 1)
    groups = n_head // splits
    patch = rows_dev * n_head
    head_index = lax.axis_index("head")
    segment = lax.axis_index("pipe")
    key_base = head_index % splits * shard_keys
    w_both = jnp.concatenate([query_weight[0], kv_weight[0]], axis=-1)
    scale_row = mod_scale[0]
    shift_row = mod_shift[0]
    gate_row = res_gate[0]

    def run_attention(valid, received, offset, keys_buf, vals_buf):

        def active(operands):
            return segment_attend(operands[0], operands[1], operands[2], operands[3], key_base)

        def resting(operands):
            return (
                operands[2],
                operands[3],
                jnp.zeros((patch, heads_dev, head_dim), jnp.float32),
                jnp.zeros((patch, heads_dev), jnp.float32),
                jnp.ones((patch, heads_dev), jnp.float32),
            )

        return lax.cond(valid, active, resting, (received, offset, keys_buf, vals_buf))

    def write_out(outputs, valid, index, updated):
        old = lax.dynamic_index_in_dim(outputs, index, 0, keepdims=False)
        return lax.dynamic_update_index_in_dim(outputs, jnp.where(valid, updated, old), index, 0)

    def entering(index, incoming):
        first = lax.dynamic_index_in_dim(patch_in, index, 0, keepdims=False)
        return jnp.where(segment == 0, first, incoming)

    outputs = jnp.zeros((micro, rows_dev, feat), jnp.bfloat16)
    incoming = jnp.zeros((rows_dev, feat), jnp.bfloat16)
    keys_buf = stale_keys[0]
    vals_buf = stale_values[0]

    def apart_step(step, carry):
        keys_buf, vals_buf, incoming, outputs = carry
        index = step - segment
        valid = (index >= 0) & (index < micro)
        safe = jnp.clip(index, 0, micro - 1)
        current = entering(safe, incoming)
        modded = modulate(current, scale_row, shift_row)
        recv_feat = lax.all_to_all(
            feature_layout(modded, groups, splits), "head", split_axis=0, concat_axis=0, tiled=True
        )
        partial_sum = project_partial(recv_feat, w_both)
        returned = lax.all_to_all(partial_sum, "head", split_axis=0, concat_axis=0, tiled=True)
        qkv_own = sum_partials(returned, groups, splits, heads_dev)
        recv_qkv = lax.all_to_all(
            head_layout(qkv_own, groups, splits), "head", split_axis=0, concat_axis=0, tiled=True
        )
        keys_buf, vals_buf, part_out, tops, totals = run_attention(
            valid, recv_qkv, patch_start[safe], keys_buf, vals_buf
        )
        outs_back, tops_back, totals_back = (
            lax.all_to_all(
                part_out.reshape(n_head, rows_dev, heads_dev * head_dim),
                "head",
                split_axis=0,
                concat_axis=0,
                tiled=True,
            ),
            lax.all_to_all(
                tops.reshape(n_head, rows_dev, heads_dev),
                "head",
                split_axis=0,
                concat_axis=0,
                tiled=True,
            ),
            lax.all_to_all(
                totals.reshape(n_head, rows_dev, heads_dev),
                "head",
                split_axis=0,
                concat_axis=0,
                tiled=True,
            ),
        )
        blended_values = merge_parts(outs_back, tops_back, totals_back, groups, splits)
        updated = (current.astype(jnp.float32) + gate_row * blended_values).astype(jnp.bfloat16)
        outputs = write_out(outputs, valid, safe, updated)
        incoming = shifted(updated, "pipe", 1)
        return (keys_buf, vals_buf, incoming, outputs)

    final = lax.fori_loop(
        0, micro + n_pipe - 1, apart_step, (keys_buf, vals_buf, incoming, outputs)
    )
    outputs = final[3]
    return outputs[None]


def solution(mesh):
    n_head = mesh.shape["head"]
    whole = n_head <= HEADS and n_head & (n_head - 1) == 0
    placed = (
        P(None, "head", None),
        P(),
        P("pipe", None),
        P("pipe", None),
        P("pipe", None),
        P("pipe", "head", None, None),
        P("pipe", "head", None, None),
        P("pipe", "head", None, None),
        P("pipe", "head", None, None),
    )
    return jax.shard_map(
        whole_heads if whole else per_device,
        mesh=mesh,
        in_specs=placed,
        out_specs=P("pipe", None, "head", None),
        check_vma=False,
    )
```

```python
import functools
import math

import jax
import jax.numpy as jnp
from jax import lax
from jax.experimental import pallas as pl
from jax.experimental.pallas import tpu as pltpu
from jax.sharding import PartitionSpec as P

HEADS = 16
MASKED = -3.0e38
LIMIT = 4 * 1024 * 1024
SMEM = pl.BlockSpec(memory_space=pltpu.SMEM)
VMEM = pl.BlockSpec(memory_space=pltpu.VMEM)
ANY = pl.BlockSpec(memory_space=pl.ANY)


def origin(head, kind, amount, count):
    if kind == "turn":
        return (head - amount + count) % count
    if kind == "ring":
        half = count // 2
        place = head // 2 + (head % 2) * (count - 1 - 2 * (head // 2))
        place = (place - amount + count) % count
        outer = place // half
        return 2 * (place + outer * (count - 1 - 2 * place)) + outer
    return head ^ amount


def traced(maps, head, count):
    for kind, amount in maps:
        head = origin(head, kind, amount, count)
    return head


def distinct(offsets, count):
    slots = {}
    for slot, maps in enumerate(offsets):
        slots.setdefault(tuple(traced(maps, head, count) for head in range(count)), (slot, maps))
    own = tuple(range(count))
    return [slots[own]] + [slots[key] for key in slots if key != own]


def routed(value, kind, amount, shift, stage, turn):
    n_pipe, n_head = lax.axis_size("pipe"), lax.axis_size("head")
    target = (stage + shift) % n_pipe
    onto = {p: (p + shift) % n_pipe for p in range(n_pipe)}
    if shift and turn > (2 if stage == 1 and shift == 1 else 1) and n_pipe % 2 == 0:
        rest = [p for p in range(n_pipe) if p not in (stage, target)]
        onto = {stage: target, target: stage}
        for first, second in zip(rest[::2], rest[1::2]):
            onto[first], onto[second] = second, first
    pairs = []
    for p in range(n_pipe):
        for h in range(n_head):
            if p == stage:
                source = origin(h, kind, amount, n_head)
            else:
                source = h if shift else origin(h, "swap", 1, n_head)
            pairs.append((p * n_head + source, onto[p] * n_head + h))
    return lax.ppermute(value, ("pipe", "head"), pairs)


def exchange(value, plan, stage, own=None, offsets=((),)):
    own = value if own is None else own
    for shift, moves in plan:
        parts, known, turn = [], [], 2 if shift < 0 else 0
        for kind, amount in moves:
            if kind == "keep":
                parts.append(own)
                known += offsets
            else:
                parts.append(routed(value, kind, amount, shift, stage, turn))
                known += [((kind, amount),) + maps for maps in offsets]
                turn += 1
        value, offsets = jnp.concatenate(parts, 0), known
        own = value
        stage = (stage + shift) % lax.axis_size("pipe")
    return value, offsets


def copied(pairs, sems):
    copies = [
        pltpu.make_async_copy(source, result, sems.at[index])
        for index, (source, result) in enumerate(pairs)
    ]
    for copy in copies:
        copy.start()
    return copies


def weight_kernel(scale_in, shift_in, gate_in, wq_in, wkv_in, own_in, *refs):
    scale_ref, shift_ref, gate_ref, weight_ref, own_ref, sems = refs
    heads_dev, _, head_dim = wq_in.shape
    width = heads_dev * head_dim
    pairs = [(own_in, own_ref)]
    for h in range(heads_dev):
        begin = h * head_dim
        pairs.append((wq_in.at[h], weight_ref.at[:, begin : begin + head_dim]))
        for part in range(2):
            begin += width
            source = wkv_in.at[h, :, part * head_dim : (part + 1) * head_dim]
            pairs.append((source, weight_ref.at[:, begin : begin + head_dim]))
    pairs += [(scale_in, scale_ref), (shift_in, shift_ref), (gate_in, gate_ref)]
    for copy in copied(pairs, sems):
        copy.wait()


def cache_kernel(micro, patch, start_in, key_in, val_in, after_ref, *refs):
    key_ref, val_ref, hidden_ref, start_ref, sems = refs
    heads_dev, _, head_dim = key_in.shape
    pairs = [(start_in, start_ref)]
    for h in range(heads_dev):
        lanes = slice(h * head_dim, (h + 1) * head_dim)
        pairs.append((key_in.at[h], key_ref.at[:, lanes]))
        pairs.append((val_in.at[h], val_ref.at[:, lanes]))
    copies = copied(pairs, sems)
    copies[0].wait()
    position = lax.broadcasted_iota(jnp.int32, hidden_ref.shape, 1)
    patch_row = lax.rem(lax.broadcasted_iota(jnp.int32, hidden_ref.shape, 0), micro)
    hidden = jnp.zeros(hidden_ref.shape, jnp.int32)
    for m in range(micro):
        relative = position - start_ref[m]
        inside = (relative >= 0) & (relative < patch) & (patch_row >= m)
        hidden = jnp.where(inside, 1, hidden)
    hidden_ref[...] = hidden
    for copy in copies[1:]:
        copy.wait()


def loaded(kernel, arrays, shapes, scratch, copies, cost, after=()):
    return pl.pallas_call(
        kernel,
        out_shape=[pltpu.VMEM(shape, dtype) for shape, dtype in shapes],
        in_specs=[ANY] * (len(arrays) + len(after)),
        out_specs=[VMEM] * len(shapes),
        scratch_shapes=scratch + [pltpu.SemaphoreType.DMA((copies,))],
        compiler_params=pltpu.CompilerParams(vmem_limit_bytes=LIMIT),
        cost_estimate=pl.CostEstimate(flops=0, bytes_accessed=cost, transcendentals=0),
    )(*(pltpu.with_memory_space_constraint(array, pltpu.HBM) for array in arrays), *after)


def layer_kernel(step, slots, micro, head_dim, *refs):
    scale_ref, shift_ref, gate_ref, weight_ref, key_ref, val_ref, hidden_ref, held_ref, in_ref, out_ref = refs[:10]
    stage = lax.axis_index("pipe")
    head = lax.axis_index("head")
    n_head = lax.axis_size("head")
    feat, positions = weight_ref.shape[0], key_ref.shape[0]
    rows, width = held_ref.shape
    heads_dev = width // head_dim
    by_token = len(in_ref.shape) == 3
    scaled_ref, order_ref = refs[10:]
    own = pl.multiple_of(head * width, width)

    @pl.when(stage != step)
    def _():
        out_ref[...] = held_ref[...].reshape(out_ref.shape)

    @pl.when(stage == step)
    def _():
        pieces = []
        if by_token:
            for index in range(n_head):
                at = index * width
                pieces.append((at, in_ref[:, :, at : at + width].astype(jnp.float32).reshape(rows, width)))
            residual = in_ref[:, :, pl.ds(own, width)].astype(jnp.float32).reshape(rows, width)
        else:
            for slot, maps in slots:
                at = pl.multiple_of(traced(maps, head, n_head) * width, width)
                pieces.append((at, in_ref[slot * rows : (slot + 1) * rows, :]))
            residual = pieces[0][1]
        square = None
        for at, piece in pieces:
            value = piece.astype(jnp.float32)
            square = value * value if square is None else square + value * value
            scaled = value * (1.0 + scale_ref[:, pl.ds(at, width)])
            scaled_ref[:rows, pl.ds(at, width)] = scaled.astype(jnp.bfloat16)
        scaled_ref[rows:, :] = jnp.broadcast_to(shift_ref[...].astype(jnp.bfloat16), (16, feat))
        projected = jnp.dot(scaled_ref[...], weight_ref[...], preferred_element_type=jnp.float32)
        inverse = lax.rsqrt(jnp.sum(square, axis=-1, keepdims=True) / feat + 1e-06)
        projected = (projected[:rows] * inverse + projected[rows : rows + 1]).astype(jnp.bfloat16)
        query, fresh_keys, fresh_vals = (projected[:, part * width : (part + 1) * width] for part in range(3))
        lane_head = lax.broadcasted_iota(jnp.int32, (rows, width), 1) // head_dim
        queries = jnp.concatenate(
            [jnp.where(lane_head == h, query, jnp.zeros_like(query)) for h in range(heads_dev)], axis=0
        )
        asked_rows = heads_dev * rows
        hidden = hidden_ref[...] != 0
        asking = lax.rem(lax.broadcasted_iota(jnp.int32, (asked_rows, rows), 0), micro)
        asked = lax.rem(lax.broadcasted_iota(jnp.int32, (asked_rows, rows), 1), micro)
        later = asked > asking
        score_scale = 1.0 / math.sqrt(head_dim)
        over_last = (((1,), (1,)), ((), ()))
        old = lax.dot_general(queries, key_ref[...], over_last, preferred_element_type=jnp.float32)
        old = old.reshape(asked_rows // 8, 8, positions) * score_scale
        old = jnp.where(hidden[None], MASKED, old).reshape(asked_rows, positions)
        new = lax.dot_general(queries, fresh_keys, over_last, preferred_element_type=jnp.float32)
        new = jnp.where(later, MASKED, new * score_scale)
        top = jnp.maximum(jnp.max(old, axis=-1, keepdims=True), jnp.max(new, axis=-1, keepdims=True))
        old = jnp.exp(old - top)
        new = jnp.exp(new - top)
        total = jnp.sum(old, axis=-1, keepdims=True) + jnp.sum(new, axis=-1, keepdims=True)
        summed = jnp.dot(
            old.astype(jnp.bfloat16), val_ref[...], preferred_element_type=jnp.float32
        ) + jnp.dot(new.astype(jnp.bfloat16), fresh_vals, preferred_element_type=jnp.float32)
        averaged = summed / total
        attended = [
            averaged[h * rows : (h + 1) * rows, h * head_dim : (h + 1) * head_dim] for h in range(heads_dev)
        ]
        gate = gate_ref[:, pl.ds(own, width)]
        result = residual.astype(jnp.float32) + gate * jnp.concatenate(attended, axis=1)
        if by_token:
            part = rows // n_head
            for slot, maps in slots:
                order_ref[traced(maps, head, n_head)] = result[slot * part : (slot + 1) * part, :]
            result = order_ref[...].reshape(rows, width)
        out_ref[...] = result.reshape(out_ref.shape).astype(out_ref.dtype)


def run_layer(step, slots, micro, head_dim, constants, held, blocks, out_shape):
    rows, width = held.shape
    n_head = lax.axis_size("head")
    return pl.pallas_call(
        functools.partial(layer_kernel, step, slots, micro, head_dim),
        out_shape=jax.ShapeDtypeStruct(out_shape, held.dtype),
        in_specs=[VMEM] * (len(constants) + 2),
        out_specs=VMEM,
        scratch_shapes=[
            pltpu.VMEM((rows + 16, n_head * width), jnp.bfloat16),
            pltpu.VMEM((n_head, rows // n_head, width), jnp.float32),
        ],
        compiler_params=pltpu.CompilerParams(vmem_limit_bytes=LIMIT),
    )(*(pltpu.with_memory_space_constraint(array, pltpu.VMEM) for array in constants), held, blocks)


def plans(n_head):
    keep = ("keep", 0)
    far = sorted(range(2, n_head, 2), key=lambda k: (k != n_head // 2, -k))
    far = tuple(("swap", k) for k in far)
    entry = ((0, (keep, ("swap", 1))), (-1, (keep,) + far))
    return entry, ((1, tuple(("swap", k) for k in range(n_head - 1, -1, -1))),)


def whole_heads(
    patch_in, patch_start, mod_scale, mod_shift, res_gate, query_weight, kv_weight, stale_keys, stale_values
):
    n_head = lax.axis_size("head")
    n_pipe = lax.axis_size("pipe")
    micro, rows_dev, feat = patch_in.shape
    heads_dev, head_dim = stale_keys.shape[1], stale_keys.shape[3]
    width = heads_dev * head_dim
    patch = rows_dev * n_head
    rows = micro * patch
    entry_plan, step_plan = plans(n_head)
    mine = jnp.transpose(patch_in, (1, 0, 2)).reshape(1, rows // n_head, feat)
    positions = stale_keys.shape[2]
    row, half = (mod_scale.shape, mod_scale.dtype), jnp.bfloat16
    *params, own = loaded(
        weight_kernel,
        (mod_scale, mod_shift, res_gate, query_weight[0], kv_weight[0], mine),
        [row] * 3 + [((feat, 3 * width), half), (mine.shape, half)],
        [],
        4 + 3 * heads_dev,
        6 * feat * 3 * width,
    )
    value, offsets = exchange(mine, entry_plan[:1], 1, own)
    caches = loaded(
        functools.partial(cache_kernel, micro, patch),
        (patch_start, stale_keys[0], stale_values[0]),
        [((positions, width), half)] * 2 + [((8, positions), jnp.int32)],
        [pltpu.SMEM(patch_start.shape, patch_start.dtype)],
        1 + 2 * heads_dev,
        6 * positions * 2 * width,
        (value,),
    )
    value, offsets = exchange(value, entry_plan[1:], 1, offsets=offsets)
    constants = (*params, *caches)
    held = jnp.zeros((rows, width), jnp.bfloat16)
    for step in range(n_pipe):
        out_shape = held.shape
        held = run_layer(step, distinct(offsets, n_head), micro, head_dim, constants, held, value, out_shape)
        if step + 1 < n_pipe:
            value, offsets = exchange(held, step_plan, step)
    back = lax.all_to_all(held, "head", split_axis=0, concat_axis=0, tiled=True)
    back = jnp.transpose(back.reshape(n_head, rows_dev, micro, width), (2, 1, 0, 3))
    return back.reshape(1, micro, rows_dev, feat)


def shifted(value, axis, steps):
    count = lax.axis_size(axis)
    leading, last = (max(0, -steps), min(count, count - steps))
    return lax.ppermute(value, axis, [(source, source + steps) for source in range(leading, last)])


def modulate(rows, scale_row, shift_row):
    values = rows.astype(jnp.float32)
    meansq = jnp.mean(values * values, axis=-1, keepdims=True)
    normed = values * lax.rsqrt(meansq + 1e-06)
    return (normed * (1.0 + scale_row) + shift_row).astype(jnp.bfloat16)


def feature_layout(modded, groups, splits):
    rows_dev, feat = modded.shape
    width = feat // splits
    pieces = jnp.transpose(modded.reshape(rows_dev, splits, width), (1, 0, 2))
    copies = jnp.broadcast_to(pieces[None], (groups, splits, rows_dev, width))
    return copies.reshape(groups * splits, rows_dev, width)


def project_partial(received, w_both):
    n_src, rows_dev, width = received.shape
    inputs = received.reshape(n_src * rows_dev, width)
    partial_sum = jnp.einsum("pf,hfe->phe", inputs, w_both, preferred_element_type=jnp.float32)
    return partial_sum.reshape(n_src, rows_dev, -1)


def sum_partials(returned, groups, splits, heads_dev):
    n_src, rows_dev, width = returned.shape
    triple = width // heads_dev
    summed = jnp.sum(returned.reshape(groups, splits, rows_dev, heads_dev, triple), axis=1)
    ordered = jnp.transpose(summed, (1, 0, 2, 3))
    return ordered.reshape(rows_dev, groups * heads_dev, triple).astype(jnp.bfloat16)


def head_layout(qkv_own, groups, splits):
    rows_dev, heads_all, triple = qkv_own.shape
    width = heads_all // groups * triple
    grouped = jnp.transpose(qkv_own.reshape(rows_dev, groups, width), (1, 0, 2))
    copies = jnp.broadcast_to(grouped[:, None], (groups, splits, rows_dev, width))
    return copies.reshape(groups * splits, rows_dev, width)


def attend_block(query_blk, keys_buf, vals_buf):
    score_scale = 1.0 / math.sqrt(query_blk.shape[-1])
    logit_scores = (
        jnp.einsum("qhd,hkd->hqk", query_blk, keys_buf, preferred_element_type=jnp.float32)
        * score_scale
    )
    top = jnp.max(logit_scores, axis=-1)
    expo = jnp.exp(logit_scores - top[..., None])
    total = jnp.sum(expo, axis=-1)
    softmax_weight = expo.astype(jnp.bfloat16)
    blended_values = jnp.einsum(
        "hqk,hkd->qhd", softmax_weight, vals_buf, preferred_element_type=jnp.float32
    )
    partial_out = blended_values / jnp.transpose(total)[..., None]
    return (partial_out, jnp.transpose(top), jnp.transpose(total))


def segment_attend(received, offset, keys_buf, vals_buf, key_base):
    heads_dev, shard_keys, head_dim = keys_buf.shape
    patch = received.shape[0] * received.shape[1]
    triples = received.reshape(patch, heads_dev, 3 * head_dim)
    query = triples[..., :head_dim]
    fresh = triples[..., head_dim:]
    position = key_base + jnp.arange(shard_keys, dtype=jnp.int32)
    relative = position - offset
    inside = ((relative >= 0) & (relative < patch))[None, :, None]
    picked = jnp.clip(relative, 0, patch - 1)
    taken = jnp.transpose(jnp.take(fresh, picked, axis=0), (1, 0, 2))
    new_keys = jnp.where(inside, taken[..., :head_dim], keys_buf)
    new_vals = jnp.where(inside, taken[..., head_dim:], vals_buf)
    block = min(512, patch)
    blocks = query.reshape(patch // block, block, heads_dev, head_dim)
    outs, tops, totals = lax.map(lambda blk: attend_block(blk, new_keys, new_vals), blocks)
    return (
        new_keys,
        new_vals,
        outs.reshape(patch, heads_dev, head_dim),
        tops.reshape(patch, heads_dev),
        totals.reshape(patch, heads_dev),
    )


def merge_parts(outs, tops, totals, groups, splits):
    n_dev, rows_dev, width = outs.shape
    heads_dev = tops.shape[-1]
    head_dim = width // heads_dev
    outs = outs.reshape(groups, splits, rows_dev, heads_dev, head_dim)
    tops = tops.reshape(groups, splits, rows_dev, heads_dev)
    totals = totals.reshape(groups, splits, rows_dev, heads_dev)
    peak = jnp.max(tops, axis=1, keepdims=True)
    weight = jnp.exp(tops - peak) * totals
    summed = jnp.sum(weight[..., None] * outs, axis=1) / jnp.sum(weight, axis=1)[..., None]
    return jnp.transpose(summed, (1, 0, 2, 3)).reshape(rows_dev, groups * width)


def per_device(
    patch_in,
    patch_start,
    mod_scale,
    mod_shift,
    res_gate,
    query_weight,
    kv_weight,
    stale_keys,
    stale_values,
):
    n_head = lax.axis_size("head")
    n_pipe = lax.axis_size("pipe")
    micro, rows_dev, feat = patch_in.shape
    heads_dev = stale_keys.shape[1]
    shard_keys = stale_keys.shape[2]
    head_dim = stale_keys.shape[3]
    splits = max(n_head // HEADS, 1)
    groups = n_head // splits
    patch = rows_dev * n_head
    head_index = lax.axis_index("head")
    segment = lax.axis_index("pipe")
    key_base = head_index % splits * shard_keys
    w_both = jnp.concatenate([query_weight[0], kv_weight[0]], axis=-1)
    scale_row = mod_scale[0]
    shift_row = mod_shift[0]
    gate_row = res_gate[0]

    def run_attention(valid, received, offset, keys_buf, vals_buf):

        def active(operands):
            return segment_attend(operands[0], operands[1], operands[2], operands[3], key_base)

        def resting(operands):
            return (
                operands[2],
                operands[3],
                jnp.zeros((patch, heads_dev, head_dim), jnp.float32),
                jnp.zeros((patch, heads_dev), jnp.float32),
                jnp.ones((patch, heads_dev), jnp.float32),
            )

        return lax.cond(valid, active, resting, (received, offset, keys_buf, vals_buf))

    def write_out(outputs, valid, index, updated):
        old = lax.dynamic_index_in_dim(outputs, index, 0, keepdims=False)
        return lax.dynamic_update_index_in_dim(outputs, jnp.where(valid, updated, old), index, 0)

    def entering(index, incoming):
        first = lax.dynamic_index_in_dim(patch_in, index, 0, keepdims=False)
        return jnp.where(segment == 0, first, incoming)

    outputs = jnp.zeros((micro, rows_dev, feat), jnp.bfloat16)
    incoming = jnp.zeros((rows_dev, feat), jnp.bfloat16)
    keys_buf = stale_keys[0]
    vals_buf = stale_values[0]

    def apart_step(step, carry):
        keys_buf, vals_buf, incoming, outputs = carry
        index = step - segment
        valid = (index >= 0) & (index < micro)
        safe = jnp.clip(index, 0, micro - 1)
        current = entering(safe, incoming)
        modded = modulate(current, scale_row, shift_row)
        recv_feat = lax.all_to_all(
            feature_layout(modded, groups, splits), "head", split_axis=0, concat_axis=0, tiled=True
        )
        partial_sum = project_partial(recv_feat, w_both)
        returned = lax.all_to_all(partial_sum, "head", split_axis=0, concat_axis=0, tiled=True)
        qkv_own = sum_partials(returned, groups, splits, heads_dev)
        recv_qkv = lax.all_to_all(
            head_layout(qkv_own, groups, splits), "head", split_axis=0, concat_axis=0, tiled=True
        )
        keys_buf, vals_buf, part_out, tops, totals = run_attention(
            valid, recv_qkv, patch_start[safe], keys_buf, vals_buf
        )
        outs_back, tops_back, totals_back = (
            lax.all_to_all(
                part_out.reshape(n_head, rows_dev, heads_dev * head_dim),
                "head",
                split_axis=0,
                concat_axis=0,
                tiled=True,
            ),
            lax.all_to_all(
                tops.reshape(n_head, rows_dev, heads_dev),
                "head",
                split_axis=0,
                concat_axis=0,
                tiled=True,
            ),
            lax.all_to_all(
                totals.reshape(n_head, rows_dev, heads_dev),
                "head",
                split_axis=0,
                concat_axis=0,
                tiled=True,
            ),
        )
        blended_values = merge_parts(outs_back, tops_back, totals_back, groups, splits)
        updated = (current.astype(jnp.float32) + gate_row * blended_values).astype(jnp.bfloat16)
        outputs = write_out(outputs, valid, safe, updated)
        incoming = shifted(updated, "pipe", 1)
        return (keys_buf, vals_buf, incoming, outputs)

    final = lax.fori_loop(
        0, micro + n_pipe - 1, apart_step, (keys_buf, vals_buf, incoming, outputs)
    )
    outputs = final[3]
    return outputs[None]


def solution(mesh):
    n_head = mesh.shape["head"]
    whole = n_head <= HEADS and n_head & (n_head - 1) == 0
    placed = (
        P(None, "head", None),
        P(),
        P("pipe", None),
        P("pipe", None),
        P("pipe", None),
        P("pipe", "head", None, None),
        P("pipe", "head", None, None),
        P("pipe", "head", None, None),
        P("pipe", "head", None, None),
    )
    return jax.shard_map(
        whole_heads if whole else per_device,
        mesh=mesh,
        in_specs=placed,
        out_specs=P("pipe", None, "head", None),
        check_vma=False,
    )
```
